32 devices in a mesh: img: 4 (over z), txt: 8 (over y, x, core).
Axes of the slice: x: 2, y: 2, z: 4, core: 2. Of those that a mesh axis runs over, the one named last changes fastest.
Arguments:
- images: bfloat16 [10240, 1024], P('img', 'txt'), may hold values from -1.5 to 1.5
- texts: bfloat16 [10240, 1024], P('txt', 'img'), may hold values from -1.5 to 1.5
- positive: int32 [10240], P('img'), may hold values from 0 to 10239, each once
Outputs:
- mean_loss: float32 [], replicated
- image_grad: bfloat16 [10240, 1024], P('img', 'txt')
- text_grad: bfloat16 [10240, 1024], P('txt', 'img')
The draws below stay inside these ranges and needn't reach their ends.
All inputs are finite; a program needn't handle non-finite values.
Results may differ from the reference program's by a relative error of at most 0.0095.
Values may be sent and summed in bfloat16 or wider, within the bound.
No kernel may reach another device: no remote copies, remote signals or barrier semaphores. Data moves between devices by JAX's collectives and lax.ppermute only.
A program may use at most 64 MiB of HBM per device.

```python
import math
import jax
import jax.numpy as jnp
from jax import lax

D = 1024
TXT_DEV = 1280
IMG_DEV = 2560
B = 10240
N_IMG = 4
N_TXT = 8


TIED_COUNT = 4


STRENGTHS = (1.5, 2.5, 3.5, 3.0)


def entry_spread():
    return 0.17 * D ** (-0.25)


def tied_spread():
    return D ** (-0.5)


def scaled_rows(row_key, tilt):
    spread = entry_spread()
    normal_key = jax.random.fold_in(row_key, 0)
    scale_key = jax.random.fold_in(row_key, 2)
    normal_part = jnp.clip(jax.random.normal(normal_key, (B, D), jnp.float32), -4.0, 4.0)
    base_rows = normal_part
    scales = jnp.exp(jax.random.uniform(scale_key, (B,), jnp.float32, math.log(0.3), math.log(2.2)))
    row_ramp = jnp.exp(tilt * (jnp.arange(B, dtype=jnp.float32) / (B - 1) - 0.5))
    return spread * (base_rows * (scales * row_ramp)[:, None])


def tied_units(base_key):
    return tied_spread() * jax.random.uniform(jax.random.fold_in(base_key, 23), (TIED_COUNT, D), jnp.float32, -1.7, 1.7)


def closeness(strength):
    return 1.0 - 2.0 / (100.0 * strength * 0.963)


def place_texts(base_key, text_rows):
    tied_rows = tied_units(base_key)
    jitter = 0.01 * tied_spread() * jax.random.normal(jax.random.fold_in(base_key, 29), (TIED_COUNT, D), jnp.float32)
    for slot_index in range(TIED_COUNT):
        lead_row = slot_index * B // TIED_COUNT + 3
        near_row = closeness(STRENGTHS[slot_index]) * tied_rows[slot_index] + jitter[slot_index]
        text_rows = text_rows.at[lead_row].set(tied_rows[slot_index])
        text_rows = text_rows.at[lead_row + 1].set(near_row)
    return text_rows


def place_images(base_key, values):
    tied_rows = tied_units(base_key)
    jitter = 0.01 * tied_spread() * jax.random.normal(jax.random.fold_in(base_key, 31), (TIED_COUNT, D), jnp.float32)
    for slot_index in range(TIED_COUNT):
        lead_row = slot_index * B // TIED_COUNT + B // (2 * TIED_COUNT)
        strength = STRENGTHS[slot_index]
        values = values.at[lead_row].set(strength * tied_rows[slot_index])
        values = values.at[lead_row + 1].set(strength * closeness(strength) * tied_rows[slot_index] + jitter[slot_index])
    return values


def draw_texts(key, part):
    values = scaled_rows(jax.random.fold_in(key, 11), math.log(8.0))
    return place_texts(key, values).astype(jnp.bfloat16)


def draw_images(key, part):
    own_key = jax.random.fold_in(key, 5)
    values = scaled_rows(own_key, math.log(8.0))
    return place_images(key, values).astype(jnp.bfloat16)


def setup_inputs(seed: int = 0) -> dict:
    streams_of = jax.random.split(jax.random.key(seed), 4)
    images = draw_images(jax.random.fold_in(streams_of[3], 71), 0)
    texts = draw_texts(jax.random.fold_in(streams_of[3], 71), 0)
    positive = jax.random.permutation(streams_of[2], B).astype(jnp.int32)
    return dict(images=images, texts=texts, positive=positive)


logit_scale = 100.0


def reference(images, texts, positive):
    texts_wide = texts.astype(jnp.float32)
    image_blocks = images.reshape(N_IMG, IMG_DEV, D)
    target_blocks = positive.reshape(N_IMG, IMG_DEV)
    column_ids = jnp.arange(B, dtype=jnp.int32)

    def block_logits(image_block):
        return logit_scale * jnp.dot(image_block.astype(jnp.float32), texts_wide.T, preferred_element_type=jnp.float32)

    def forward(running, inputs):
        col_max, col_sum = running
        image_block, targets = inputs
        logits = block_logits(image_block)
        row_max = jnp.max(logits, axis=1)
        row_lse = row_max + jnp.log(jnp.sum(jnp.exp(logits - row_max[:, None]), axis=1))
        new_max = jnp.maximum(col_max, jnp.max(logits, axis=0))
        col_sum = col_sum * jnp.exp(col_max - new_max) + jnp.sum(jnp.exp(logits - new_max[None, :]), axis=0)
        matches = targets[:, None] == column_ids[None, :]
        picked = jnp.sum(jnp.where(matches, logits, jnp.zeros_like(logits)))
        return (new_max, col_sum), (row_lse, picked)

    initial = (jnp.full((B,), -jnp.inf, jnp.float32), jnp.zeros((B,), jnp.float32))
    (col_max, col_sum), (row_lse, picked_sums) = lax.scan(forward, initial, (image_blocks, target_blocks))
    col_lse = col_max + jnp.log(col_sum)
    mean_loss = (jnp.sum(row_lse) + jnp.sum(col_lse) - 2.0 * jnp.sum(picked_sums)) / (2.0 * B)

    text_blocks = texts_wide.reshape(N_TXT, TXT_DEV, D)

    def backward(text_total, inputs):
        image_block, targets, lse_rows = inputs
        logits = block_logits(image_block)
        matches = (targets[:, None] == column_ids[None, :]).astype(jnp.float32)
        weights = (jnp.exp(logits - lse_rows[:, None]) + jnp.exp(logits - col_lse[None, :]) - 2.0 * matches).astype(jnp.bfloat16)
        weight_blocks = weights.reshape(IMG_DEV, N_TXT, TXT_DEV).astype(jnp.float32)
        partials = logit_scale * jnp.einsum('rnc,ncd->nrd', weight_blocks, text_blocks)
        rounded = lax.optimization_barrier(partials.astype(jnp.bfloat16)).astype(jnp.float32)
        image_part = jnp.sum(rounded, axis=0).astype(jnp.bfloat16)
        text_term = logit_scale * jnp.dot(weights.astype(jnp.float32).T, image_block.astype(jnp.float32), preferred_element_type=jnp.float32)
        text_total = text_total + lax.optimization_barrier(text_term.astype(jnp.bfloat16)).astype(jnp.float32)
        return text_total, image_part

    text_total, image_parts = lax.scan(backward, jnp.zeros((B, D), jnp.float32), (image_blocks, target_blocks, row_lse))
    return mean_loss, image_parts.reshape(B, D), text_total.astype(jnp.bfloat16)
```

```python
import functools
import math
import jax
import jax.numpy as jnp
from jax import lax
from jax.experimental import pallas as pl
from jax.experimental.pallas import tpu as pltpu
from jax.sharding import PartitionSpec as P

logit_scale = 100.0
log2e = math.log2(math.e)
ln2 = math.log(2.0)
strip = 16
vmem_bytes = 28 * 1024 * 1024

VMEM = pl.BlockSpec(memory_space=pltpu.VMEM)
ANY = pl.BlockSpec(memory_space=pl.ANY)


def block_rows(rows, most):
    size = most
    while rows % size:
        size //= 2
    return size


def columns(slot, width):
    return pl.ds(pl.multiple_of(slot * width, width), width)


def params():
    return pltpu.CompilerParams(vmem_limit_bytes=vmem_bytes)


def cost(rows, cols, depth, exps):
    return pl.CostEstimate(
        flops=2 * rows * cols * depth,
        bytes_accessed=rows * cols * 4 + rows * depth * 2,
        transcendentals=rows * cols * exps,
    )


def place_pieces(pieces, width):
    rows = max(first + piece.shape[0] for piece, first, _ in pieces)

    def kernel(*refs):
        *sources, out, sems = refs
        copies = []
        for k, (source, (piece, first, slot)) in enumerate(zip(sources, pieces)):
            wide = piece.shape[1]
            target = out.at[pl.ds(first, piece.shape[0]), columns(slot(), wide)]
            copies.append(pltpu.make_async_copy(source, target, sems.at[k]))
        for copy in copies:
            copy.start()
        for copy in copies:
            copy.wait()

    return pl.pallas_call(
        kernel,
        out_shape=jax.ShapeDtypeStruct((rows, width), pieces[0][0].dtype),
        in_specs=[ANY] * len(pieces),
        out_specs=ANY,
        scratch_shapes=[pltpu.SemaphoreType.DMA((len(pieces),))],
        name="place_pieces",
    )(*[piece for piece, _, _ in pieces])


def log_add(a, b):
    larger = jnp.maximum(a, b)
    return larger + jnp.log(jnp.exp2(a - larger) + jnp.exp2(b - larger)) * log2e


def logits_and_stats(images, pieces, rows, earlier):
    img_rows, width = images.shape
    bm = block_rows(img_rows, 512)
    steps = img_rows // bm

    def kernel(*refs):
        sources = refs[: len(pieces)]
        refs = refs[len(pieces) :]
        if earlier is not None:
            earlier_ref, *refs = refs
        images_ref, u_ref, texts_ref, row_ref, col_ref, d_scr, rows_scr, cm_scr, cs_scr, sems = refs
        step = pl.program_id(0)

        @pl.when(step == 0)
        def _():
            copies = []
            for k, (source, (_, first, slot, condition)) in enumerate(zip(sources, pieces)):
                wide = source.shape[1]
                copy = pltpu.make_async_copy(
                    source.at[pl.ds(first, rows)], texts_ref.at[:, columns(slot(), wide)], sems.at[k]
                )
                if condition is None:
                    copy.start()
                else:
                    pl.when(condition())(copy.start)
                copies.append((copy, condition))
            cm_scr[...] = jnp.full(cm_scr.shape, -jnp.inf, jnp.float32)
            cs_scr[...] = jnp.zeros(cs_scr.shape, jnp.float32)
            rows_scr[...] = jnp.zeros(rows_scr.shape, jnp.float32)
            for copy, condition in copies:
                if condition is None:
                    copy.wait()
                else:
                    pl.when(condition())(copy.wait)

        d_scr[...] = lax.dot_general(
            images_ref[...], texts_ref[...], (((1,), (1,)), ((), ())), preferred_element_type=jnp.float32
        )
        lane = lax.broadcasted_iota(jnp.int32, (strip, 128), 1)

        def first_pass(s, top):
            at = pl.ds(pl.multiple_of(s * strip, strip), strip)
            u = d_scr[at, :] * (logit_scale * log2e)
            u_ref[at, :] = u
            row_max = jnp.max(u, axis=1, keepdims=True)
            row_sum = jnp.sum(jnp.exp2(u - row_max), axis=1, keepdims=True)
            row_lse = row_max + jnp.log(row_sum) * log2e
            rows_scr[at, :] = jnp.where(lane == step, row_lse, rows_scr[at, :])
            return jnp.maximum(top, jnp.max(u.reshape(strip // 8, 8, rows), axis=0))

        old = cm_scr[...]
        new = lax.fori_loop(0, bm // strip, first_pass, old, unroll=4)

        def second_pass(s, total):
            at = pl.ds(pl.multiple_of(s * strip, strip), strip)
            u = u_ref[at, :].reshape(strip // 8, 8, rows)
            return total + jnp.sum(jnp.exp2(u - new[None]), axis=0)

        total = cs_scr[...] * jnp.exp2(old - new)
        total = lax.fori_loop(0, bm // strip, second_pass, total, unroll=4)
        cm_scr[...] = new
        cs_scr[...] = total

        @pl.when(step == steps - 1)
        def _():
            top = jnp.max(new, axis=0, keepdims=True)
            col_sum = jnp.sum(total * jnp.exp2(new - top), axis=0, keepdims=True)
            col_ref[...] = top + jnp.log(col_sum) * log2e
            own = rows_scr[...].T[:8]
            row_ref[...] = own if earlier is None else log_add(own, earlier_ref[...])

    out = pl.pallas_call(
        kernel,
        grid=(steps,),
        out_shape=(
            jax.ShapeDtypeStruct((img_rows, rows), jnp.float32),
            jax.ShapeDtypeStruct((rows, width), jnp.bfloat16),
            jax.ShapeDtypeStruct((8, bm), jnp.float32),
            jax.ShapeDtypeStruct((1, rows), jnp.float32),
        ),
        in_specs=[ANY] * len(pieces)
        + ([] if earlier is None else [VMEM])
        + [pl.BlockSpec((bm, width), lambda i: (i, 0))],
        out_specs=(pl.BlockSpec((bm, rows), lambda i: (i, 0)), VMEM, VMEM, VMEM),
        scratch_shapes=[
            pltpu.VMEM((bm, rows), jnp.float32),
            pltpu.VMEM((bm, 128), jnp.float32),
            pltpu.VMEM((8, rows), jnp.float32),
            pltpu.VMEM((8, rows), jnp.float32),
            pltpu.SemaphoreType.DMA((len(pieces),)),
        ],
        compiler_params=params(),
        cost_estimate=cost(img_rows, rows, width, 2),
        name="logits_and_stats",
    )(*[p[0] for p in pieces], *([] if earlier is None else [earlier]), images)
    return out


def weights_and_text_grad(u, images, targets, row_lse, col_lse, first, parts):
    img_rows, width = images.shape
    rows = u.shape[1]
    bm = row_lse.shape[1]
    steps = img_rows // bm
    wide = width // len(parts)

    def kernel(u_ref, images_ref, targets_ref, row_ref, col_ref, w_ref, pos_ref, *refs):
        *part_refs, acc, rows_scr, pos_scr = refs
        step = pl.program_id(0)

        @pl.when(step == 0)
        def _():
            padded = jnp.concatenate([row_ref[...], jnp.zeros((120, bm), jnp.float32)], axis=0)
            rows_scr[...] = padded.T
            pos_scr[...] = jnp.zeros(pos_scr.shape, jnp.float32)

        lane = lax.broadcasted_iota(jnp.int32, (strip, 128), 1)
        ids = lax.broadcasted_iota(jnp.int32, (strip, rows), 1) + first
        col = col_ref[...]

        def one(s, picked):
            at = pl.ds(pl.multiple_of(s * strip, strip), strip)
            v = u_ref[at, :]
            row = jnp.sum(jnp.where(lane == step, rows_scr[at, :], 0.0), axis=1, keepdims=True)
            matches = targets_ref[at, :] == ids
            weight = jnp.exp2(v - row) + jnp.exp2(v - col) - jnp.where(matches, 2.0, 0.0)
            w_ref[at, :] = weight.astype(jnp.bfloat16)
            return picked + jnp.sum(jnp.where(matches, v, 0.0).reshape(strip // 8, 8, rows), axis=0)

        pos_scr[...] = lax.fori_loop(0, bm // strip, one, pos_scr[...], unroll=4)
        term = lax.dot_general(
            w_ref[...], images_ref[...], (((0,), (0,)), ((), ())), preferred_element_type=jnp.float32
        )

        @pl.when(step == 0)
        def _():
            acc[...] = term

        @pl.when(step > 0)
        def _():
            acc[...] += term

        @pl.when(step == steps - 1)
        def _():
            for ref, slot in zip(part_refs, parts):
                ref[...] = (logit_scale * acc[:, columns(slot(), wide)]).astype(jnp.bfloat16)
            pos_ref[...] = jnp.sum(pos_scr[...], axis=0, keepdims=True)

    return pl.pallas_call(
        kernel,
        grid=(steps,),
        out_shape=(
            jax.ShapeDtypeStruct((img_rows, rows), jnp.bfloat16),
            jax.ShapeDtypeStruct((1, rows), jnp.float32),
        )
        + (jax.ShapeDtypeStruct((rows, wide), jnp.bfloat16),) * len(parts),
        in_specs=[
            pl.BlockSpec((bm, rows), lambda i: (i, 0)),
            pl.BlockSpec((bm, width), lambda i: (i, 0)),
            pl.BlockSpec((bm, 1), lambda i: (i, 0)),
            VMEM,
            VMEM,
        ],
        out_specs=(pl.BlockSpec((bm, rows), lambda i: (i, 0)), VMEM) + (VMEM,) * len(parts),
        scratch_shapes=[
            pltpu.VMEM((rows, width), jnp.float32),
            pltpu.VMEM((bm, 128), jnp.float32),
            pltpu.VMEM((8, rows), jnp.float32),
        ],
        compiler_params=params(),
        cost_estimate=cost(img_rows, rows, width, 2),
        name="weights_and_text_grad",
    )(u, images, targets, row_lse, col_lse)


def image_grad_parts(weights, texts, first, img_rows, groups):
    width = texts[0].shape[1]
    rows = texts[0].shape[0]
    bm = block_rows(math.gcd(first, img_rows) if first else img_rows, 256)
    wide = width // sum(len(g) for g in groups)

    def kernel(*refs):
        w_refs = refs[: len(weights)]
        t_refs = refs[len(weights) : 2 * len(weights)]
        *outs, acc = refs[2 * len(weights) :]
        total = jnp.dot(w_refs[0][...], t_refs[0][...], preferred_element_type=jnp.float32)
        for w_ref, t_ref in zip(w_refs[1:], t_refs[1:]):
            total += jnp.dot(w_ref[...], t_ref[...], preferred_element_type=jnp.float32)
        acc[...] = logit_scale * total
        for out, group in zip(outs, groups):
            for k, slot in enumerate(group):
                out[:, k * wide : (k + 1) * wide] = acc[:, columns(slot(), wide)].astype(jnp.bfloat16)

    return pl.pallas_call(
        kernel,
        grid=(img_rows // bm,),
        out_shape=tuple(jax.ShapeDtypeStruct((img_rows, wide * len(g)), jnp.bfloat16) for g in groups),
        in_specs=[pl.BlockSpec((bm, rows), lambda i: (i + first // bm, 0))] * len(weights)
        + [VMEM] * len(weights),
        out_specs=tuple(pl.BlockSpec((bm, wide * len(g)), lambda i: (i, 0)) for g in groups),
        scratch_shapes=[pltpu.VMEM((bm, width), jnp.float32)],
        compiler_params=params(),
        cost_estimate=cost(img_rows, rows * len(weights), width, 0),
        name="image_grad_parts",
    )(*weights, *texts)


def loss_of(row_lse, col_lses, picked, img_rows, pairs, n_img, n_txt):
    bm = row_lse.shape[1]
    row_term = jnp.sum(row_lse[: img_rows // bm])
    col_term = sum(jnp.sum(c) for c in col_lses)
    pos = sum(jnp.sum(p) for p in picked)
    total = lax.psum(row_term / n_txt + col_term / n_img - 2.0 * pos, ("img", "txt"))
    return total * (ln2 / (2.0 * pairs))


def shifted(count, by, wrap):
    return [(i, (i + by) % count) for i in range(count) if wrap or 0 <= i + by < count]


def paired(count, by):
    return [(i, i ^ by) for i in range(count)]


def per_device_4x8(images, texts, positive):
    img_rows = images.shape[0]
    txt_rows, quarter = texts.shape
    width = quarter * 4
    half = txt_rows // 2
    up_ring, down_ring = shifted(4, 1, True), shifted(4, -1, True)
    up_line, down_line = [(1, 2), (2, 3)], [(1, 0), (2, 1)]

    def swap(part, by):
        return lax.ppermute(part, "txt", paired(8, by))

    def z_gather(part):
        prev = lax.ppermute(part, "img", up_ring)
        following = lax.ppermute(part, "img", down_ring)
        return prev, following, lax.ppermute(prev, "img", up_line), lax.ppermute(following, "img", down_line)

    gathered = [z_gather(texts[:half]), z_gather(texts[half:])]
    image_half = img_rows // 2
    from_x, from_y = swap(images, 2), swap(images, 4)
    diag_x, diag_y = swap(from_y[:image_half], 2), swap(from_x[image_half:], 4)
    mine = [(images, 0, 0), (from_x, 0, 2), (from_y, 0, 4), (diag_x, 0, 6), (diag_y, image_half, 6)]
    pieces = mine + [(swap(part, 1), first, flip ^ 1) for part, first, flip in mine]

    def txt_slot(flip):
        return lambda: lax.axis_index("txt") ^ flip

    def img_slot(by):
        return lambda: lax.rem(lax.axis_index("img") + by, 4)

    def upper():
        return lax.axis_index("img") >= 2

    def lower():
        return lax.axis_index("img") < 2

    whole_img = place_pieces([(part, first, txt_slot(flip)) for part, first, flip in pieces], width)
    targets = (positive - lax.axis_index("txt") * txt_rows)[:, None]

    def text_pieces(k):
        prev, following, up, down = gathered[k]
        return [
            (texts, k * half, img_slot(0), None),
            (prev, 0, img_slot(3), None),
            (following, 0, img_slot(1), None),
            (up, 0, img_slot(2), upper),
            (down, 0, img_slot(2), lower),
        ]

    def over_img(col):
        col = log_add(col, lax.ppermute(col, "img", paired(4, 1)))
        return log_add(col, lax.ppermute(col, "img", paired(4, 2)))

    u0, texts0, row, col0 = logits_and_stats(whole_img, text_pieces(0), half, None)
    col0 = over_img(col0)
    u1, texts1, row, col1 = logits_and_stats(whole_img, text_pieces(1), half, row)
    for by in (1, 2, 4):
        row = log_add(row, swap(row, by))
    col1 = over_img(col1)

    text_slots = [img_slot(2), img_slot(1), img_slot(3), img_slot(0)]
    weights, picked, text_parts = [], [], []
    for k, (u, col) in enumerate(((u0, col0), (u1, col1))):
        w, pos, opposite, following, prev, own = weights_and_text_grad(
            u, whole_img, targets, row, col, k * half, text_slots
        )
        weights.append(w)
        picked.append(pos)
        from_below = lax.ppermute(opposite, "img", [(0, 1), (1, 2)])
        from_above = lax.ppermute(opposite, "img", [(3, 2), (2, 1)])
        from_prev = lax.ppermute(following + from_below, "img", up_ring)
        from_next = lax.ppermute(prev + from_above, "img", down_ring)
        text_parts.append(
            (own.astype(jnp.float32) + from_prev.astype(jnp.float32) + from_next.astype(jnp.float32)).astype(
                jnp.bfloat16
            )
        )
    text_grad = jnp.concatenate(text_parts, axis=0)
    mean_loss = loss_of(row, (col0, col1), picked, img_rows, txt_rows * 8, 4, 8)

    kept = [[txt_slot(0)], [txt_slot(2)], [txt_slot(4)], [txt_slot(6)]]
    sent = [txt_slot(flip) for flip in (1, 3, 5, 7)]
    sums = []
    eighth = width // 8
    for k in range(2):
        *own, other = image_grad_parts(weights, (texts0, texts1), k * image_half, image_half, kept + [sent])
        other = swap(other, 1)
        sums.append([own[j] + other[:, j * eighth : (j + 1) * eighth] for j in range(4)])
    (s0, x0, y0, d0), (s1, x1, y1, d1) = sums
    d0 = swap(d0, 2)
    d1 = swap(d1, 4)
    image_parts = []
    for s, x, y in ((s0, x0, y0 + d0), (s1, x1 + d1, y1)):
        x, y = swap(x, 2), swap(y, 4)
        image_parts.append(
            (s.astype(jnp.float32) + x.astype(jnp.float32) + y.astype(jnp.float32)).astype(jnp.bfloat16)
        )
    return mean_loss, jnp.concatenate(image_parts, axis=0), text_grad


def per_device(images, texts, positive):
    n_img, n_txt = lax.axis_size("img"), lax.axis_size("txt")
    if (n_img, n_txt) == (4, 8):
        return per_device_4x8(images, texts, positive)
    whole_img = lax.all_gather(images, "txt", axis=1, tiled=True)
    whole_txt = lax.all_gather(texts, "img", axis=1, tiled=True)
    img_rows = whole_img.shape[0]
    txt_rows = whole_txt.shape[0]
    half = txt_rows // 2
    targets = (positive - lax.axis_index("txt") * txt_rows)[:, None]

    def merged(part, axis):
        every = lax.all_gather(part, axis)
        top = jnp.max(every, axis=0)
        return top + jnp.log(jnp.sum(jnp.exp2(every - top), axis=0)) * log2e

    def first_slot():
        return jnp.int32(0)

    row, logits, chunks, cols = None, [], [], []
    for k in range(2):
        u, chunk, row, col = logits_and_stats(whole_img, [(whole_txt, k * half, first_slot, None)], half, row)
        logits.append(u)
        chunks.append(chunk)
        cols.append(merged(col, "img"))
    row = merged(row, "txt")
    weights, picked, text_parts = [], [], []
    for k in range(2):
        w, pos, part = weights_and_text_grad(logits[k], whole_img, targets, row, cols[k], k * half, [first_slot])
        weights.append(w)
        picked.append(pos)
        text_parts.append(part)
    (image_part,) = image_grad_parts(weights, chunks, 0, img_rows, [[first_slot]])
    mean_loss = loss_of(row, cols, picked, img_rows, txt_rows * n_txt, n_img, n_txt)
    image_grad = lax.psum_scatter(image_part, "txt", scatter_dimension=1, tiled=True)
    text_grad = lax.psum_scatter(jnp.concatenate(text_parts, axis=0), "img", scatter_dimension=1, tiled=True)
    return mean_loss, image_grad, text_grad


def solution(mesh):
    placed = (P("img", "txt"), P("txt", "img"), P("img"))
    return jax.shard_map(
        per_device,
        mesh=mesh,
        in_specs=placed,
        out_specs=(P(), P("img", "txt"), P("txt", "img")),
        check_vma=False,
    )
```

```python
import functools
import math
import jax
import jax.numpy as jnp
from jax import lax
from jax.experimental import pallas as pl
from jax.experimental.pallas import tpu as pltpu
from jax.sharding import PartitionSpec as P

logit_scale = 100.0
log2e = math.log2(math.e)
ln2 = math.log(2.0)
strip = 32
vmem_bytes = 28 * 1024 * 1024

VMEM = pl.BlockSpec(memory_space=pltpu.VMEM)


def block_rows(rows, most):
    size = most
    while rows % size:
        size //= 2
    return size


def columns(slot, width):
    return pl.ds(pl.multiple_of(slot * width, width), width)


def params():
    return pltpu.CompilerParams(vmem_limit_bytes=vmem_bytes)


def cost(rows, cols, depth, exps):
    return pl.CostEstimate(
        flops=2 * rows * cols * depth,
        bytes_accessed=rows * cols * 4 + rows * depth * 2,
        transcendentals=rows * cols * exps,
    )


def place_pieces(pieces, half, width):
    rows = pieces[0][0].shape[0]
    wide = pieces[0][0].shape[1]
    bm = block_rows(half, 256)
    near = half // bm
    arrays, specs = [], []
    for upper, lower, _ in pieces:
        if lower is None:
            arrays.append(upper)
            specs.append(pl.BlockSpec((bm, wide), lambda i: (i, 0)))
        else:
            arrays.append(upper)
            specs.append(pl.BlockSpec((bm, wide), lambda i: (jnp.minimum(i, near - 1), 0)))
            arrays.append(lower)
            specs.append(pl.BlockSpec((bm, wide), lambda i: (jnp.maximum(i - near, 0), 0)))

    def kernel(*refs):
        *sources, out = refs
        step = pl.program_id(0)
        at = 0
        for _, lower, slot in pieces:
            if lower is None:
                out[:, columns(slot(), wide)] = sources[at][...]
                at += 1
            else:
                out[:, columns(slot(), wide)] = jnp.where(step < near, sources[at][...], sources[at + 1][...])
                at += 2

    return pl.pallas_call(
        kernel,
        grid=(rows // bm,),
        out_shape=jax.ShapeDtypeStruct((rows, width), pieces[0][0].dtype),
        in_specs=specs,
        out_specs=pl.BlockSpec((bm, width), lambda i: (i, 0)),
        compiler_params=params(),
        name="place_pieces",
    )(*arrays)


def log_add(a, b):
    larger = jnp.maximum(a, b)
    return larger + jnp.log(jnp.exp2(a - larger) + jnp.exp2(b - larger)) * log2e


def lanes(x):
    return [x[:, k : k + 128] for k in range(0, x.shape[1], 128)]


def logits_and_stats(images, pieces, rows, earlier):
    img_rows, width = images.shape
    bm = block_rows(img_rows, 512)
    steps = img_rows // bm

    def kernel(*refs):
        sources = refs[: len(pieces)]
        refs = refs[len(pieces) :]
        if earlier is not None:
            earlier_ref, *refs = refs
        images_ref, u_ref, texts_ref, row_ref, col_ref, d_scr, rm_scr, rs_scr, cm_scr, cs_scr = refs
        step = pl.program_id(0)

        @pl.when(step == 0)
        def _():
            for source, (_, first, slot, condition) in zip(sources, pieces):

                def copy(source=source, first=first, slot=slot):
                    texts_ref[:, columns(slot(), source.shape[1])] = source[pl.ds(first, rows), :]

                if condition is None:
                    copy()
                else:
                    pl.when(condition())(copy)
            cm_scr[...] = jnp.full(cm_scr.shape, -jnp.inf, jnp.float32)
            cs_scr[...] = jnp.zeros(cs_scr.shape, jnp.float32)

        d_scr[...] = lax.dot_general(
            images_ref[...], texts_ref[...], (((1,), (1,)), ((), ())), preferred_element_type=jnp.float32
        )

        def first_pass(s, top):
            at = pl.ds(pl.multiple_of(s * strip, strip), strip)
            u = d_scr[at, :] * (logit_scale * log2e)
            u_ref[at, :] = u
            rm_scr[at, :] = functools.reduce(jnp.maximum, lanes(u))
            return jnp.maximum(top, jnp.max(u.reshape(strip // 8, 8, rows), axis=0))

        old = cm_scr[...]
        new = lax.fori_loop(0, bm // strip, first_pass, old, unroll=2)

        def second_pass(s, total):
            at = pl.ds(pl.multiple_of(s * strip, strip), strip)
            u = u_ref[at, :]
            row_max = rm_scr[at, :]
            rs_scr[at, :] = functools.reduce(jnp.add, [jnp.exp2(v - row_max) for v in lanes(u)])
            return total + jnp.sum(jnp.exp2(u.reshape(strip // 8, 8, rows) - new[None]), axis=0)

        total = lax.fori_loop(0, bm // strip, second_pass, cs_scr[...] * jnp.exp2(old - new), unroll=2)
        cm_scr[...] = new
        cs_scr[...] = total
        lane_max = rm_scr[...].T
        top_row = jnp.max(lane_max, axis=0, keepdims=True)
        row_sum = jnp.sum(rs_scr[...].T * jnp.exp2(lane_max - top_row), axis=0, keepdims=True)
        row_lse = top_row + jnp.log(row_sum) * log2e
        if earlier is not None:
            row_lse = log_add(row_lse, earlier_ref[pl.ds(step, 1), :])
        row_ref[pl.ds(step, 1), :] = row_lse

        @pl.when(step == steps - 1)
        def _():
            top = jnp.max(new, axis=0, keepdims=True)
            col_sum = jnp.sum(total * jnp.exp2(new - top), axis=0, keepdims=True)
            col_ref[...] = top + jnp.log(col_sum) * log2e

    return pl.pallas_call(
        kernel,
        grid=(steps,),
        out_shape=(
            jax.ShapeDtypeStruct((img_rows, rows), jnp.float32),
            jax.ShapeDtypeStruct((rows, width), jnp.bfloat16),
            jax.ShapeDtypeStruct((steps, bm), jnp.float32),
            jax.ShapeDtypeStruct((1, rows), jnp.float32),
        ),
        in_specs=[VMEM] * len(pieces)
        + ([] if earlier is None else [VMEM])
        + [pl.BlockSpec((bm, width), lambda i: (i, 0))],
        out_specs=(pl.BlockSpec((bm, rows), lambda i: (i, 0)), VMEM, VMEM, VMEM),
        scratch_shapes=[
            pltpu.VMEM((bm, rows), jnp.float32),
            pltpu.VMEM((bm, 128), jnp.float32),
            pltpu.VMEM((bm, 128), jnp.float32),
            pltpu.VMEM((8, rows), jnp.float32),
            pltpu.VMEM((8, rows), jnp.float32),
        ],
        compiler_params=params(),
        cost_estimate=cost(img_rows, rows, width, 2),
        name="logits_and_stats",
    )(*[p[0] for p in pieces], *([] if earlier is None else [earlier]), images)


def weights_and_text_grad(u, images, targets, row_lse, col_lse, first, parts):
    img_rows, width = images.shape
    rows = u.shape[1]
    bm = row_lse.shape[1]
    steps = img_rows // bm
    wide = width // len(parts)

    def kernel(u_ref, images_ref, targets_ref, row_ref, col_ref, w_ref, pos_ref, *refs):
        *part_refs, acc, row_scr, target_scr, pos_scr = refs
        step = pl.program_id(0)
        row_scr[...] = jnp.broadcast_to(row_ref[pl.ds(step, 1), :], (128, bm)).T
        target_scr[...] = jnp.broadcast_to(targets_ref[pl.ds(step, 1), :] - first, (128, bm)).T

        @pl.when(step == 0)
        def _():
            pos_scr[...] = jnp.zeros(pos_scr.shape, jnp.float32)

        ids = lax.broadcasted_iota(jnp.int32, (strip, 128), 1)
        col = col_ref[...]

        def one(s, picked):
            at = pl.ds(pl.multiple_of(s * strip, strip), strip)
            row = row_scr[at, :]
            target = target_scr[at, :] - ids
            for k in range(0, rows, 128):
                v = u_ref[at, k : k + 128]
                matches = target == k
                weight = jnp.exp2(v - row) + jnp.exp2(v - col[:, k : k + 128]) - jnp.where(matches, 2.0, 0.0)
                w_ref[at, k : k + 128] = weight.astype(jnp.bfloat16)
                picked = picked + jnp.where(matches, v, 0.0)
            return picked

        pos_scr[...] = lax.fori_loop(0, bm // strip, one, pos_scr[...], unroll=2)
        term = lax.dot_general(
            w_ref[...], images_ref[...], (((0,), (0,)), ((), ())), preferred_element_type=jnp.float32
        )

        @pl.when(step == 0)
        def _():
            acc[...] = term

        @pl.when(step > 0)
        def _():
            acc[...] += term

        @pl.when(step == steps - 1)
        def _():
            for ref, slot in zip(part_refs, parts):
                ref[...] = (logit_scale * acc[:, columns(slot(), wide)]).astype(jnp.bfloat16)
            pos_ref[...] = jnp.sum(pos_scr[...], axis=0, keepdims=True)

    return pl.pallas_call(
        kernel,
        grid=(steps,),
        out_shape=(
            jax.ShapeDtypeStruct((img_rows, rows), jnp.bfloat16),
            jax.ShapeDtypeStruct((1, 128), jnp.float32),
        )
        + (jax.ShapeDtypeStruct((rows, wide), jnp.bfloat16),) * len(parts),
        in_specs=[
            pl.BlockSpec((bm, rows), lambda i: (i, 0)),
            pl.BlockSpec((bm, width), lambda i: (i, 0)),
            VMEM,
            VMEM,
            VMEM,
        ],
        out_specs=(pl.BlockSpec((bm, rows), lambda i: (i, 0)), VMEM) + (VMEM,) * len(parts),
        scratch_shapes=[
            pltpu.VMEM((rows, width), jnp.float32),
            pltpu.VMEM((bm, 128), jnp.float32),
            pltpu.VMEM((bm, 128), jnp.int32),
            pltpu.VMEM((strip, 128), jnp.float32),
        ],
        compiler_params=params(),
        cost_estimate=cost(img_rows, rows, width, 2),
        name="weights_and_text_grad",
    )(u, images, targets, row_lse, col_lse)


def image_grad_parts(weights, texts, first, img_rows, groups):
    width = texts[0].shape[1]
    rows = sum(t.shape[0] for t in texts)
    bm = block_rows(math.gcd(first, img_rows) if first else img_rows, 256)
    wide = width // sum(len(g) for g in groups)

    def kernel(*refs):
        w_refs = refs[: len(weights)]
        t_refs = refs[len(weights) : 2 * len(weights)]
        *outs, acc = refs[2 * len(weights) :]
        total = jnp.dot(w_refs[0][...], t_refs[0][...], preferred_element_type=jnp.float32)
        for w_ref, t_ref in zip(w_refs[1:], t_refs[1:]):
            total += jnp.dot(w_ref[...], t_ref[...], preferred_element_type=jnp.float32)
        acc[...] = logit_scale * total
        for out, group in zip(outs, groups):
            for k, slot in enumerate(group):
                out[:, k * wide : (k + 1) * wide] = acc[:, columns(slot(), wide)].astype(jnp.bfloat16)

    return pl.pallas_call(
        kernel,
        grid=(img_rows // bm,),
        out_shape=tuple(jax.ShapeDtypeStruct((img_rows, wide * len(g)), jnp.bfloat16) for g in groups),
        in_specs=[pl.BlockSpec((bm, w.shape[1]), lambda i: (i + first // bm, 0)) for w in weights]
        + [VMEM] * len(weights),
        out_specs=tuple(pl.BlockSpec((bm, wide * len(g)), lambda i: (i, 0)) for g in groups),
        scratch_shapes=[pltpu.VMEM((bm, width), jnp.float32)],
        compiler_params=params(),
        cost_estimate=cost(img_rows, rows, width, 0),
        name="image_grad_parts",
    )(*weights, *texts)


def loss_terms(row_lse, col_lses, picked, n_img, n_txt):
    pos = sum(jnp.sum(p) for p in picked)
    return jnp.sum(row_lse) / n_txt + sum(jnp.sum(c) for c in col_lses) / n_img - 2.0 * pos


def chunk_rows(rows):
    units = rows // 256
    first = (units + 1) // 2 * 256 if rows % 256 == 0 and units > 1 else rows // 2
    return first, rows - first


def shifted(count, by, wrap):
    return [(i, (i + by) % count) for i in range(count) if wrap or 0 <= i + by < count]


def paired(count, by):
    return [(i, i ^ by) for i in range(count)]


def per_device_4x8(images, texts, positive):
    img_rows = images.shape[0]
    txt_rows, quarter = texts.shape
    width = quarter * 4
    chunks = chunk_rows(txt_rows)
    firsts = (0, chunks[0])
    up_ring, down_ring = shifted(4, 1, True), shifted(4, -1, True)
    up_line, down_line = [(1, 2), (2, 3)], [(1, 0), (2, 1)]

    def swap(part, by):
        return lax.ppermute(part, "txt", paired(8, by))

    def z_gather(part):
        prev = lax.ppermute(part, "img", up_ring)
        following = lax.ppermute(part, "img", down_ring)
        return prev, following, lax.ppermute(prev, "img", up_line), lax.ppermute(following, "img", down_line)

    gathered = [z_gather(texts[f : f + c]) for f, c in zip(firsts, chunks)]
    image_half = img_rows // 2
    from_x, from_y = swap(images, 2), swap(images, 4)
    diag_x, diag_y = swap(from_y[:image_half], 2), swap(from_x[image_half:], 4)
    mine = [(images, None, 0), (from_x, None, 2), (from_y, None, 4), (diag_x, diag_y, 6)]
    pieces = mine + [
        (swap(upper, 1), None if lower is None else swap(lower, 1), flip ^ 1) for upper, lower, flip in mine
    ]

    def txt_slot(flip):
        return lambda: lax.axis_index("txt") ^ flip

    def img_slot(by):
        return lambda: lax.rem(lax.axis_index("img") + by, 4)

    def upper():
        return lax.axis_index("img") >= 2

    def lower():
        return lax.axis_index("img") < 2

    whole_img = place_pieces([(a, b, txt_slot(flip)) for a, b, flip in pieces], image_half, width)

    def text_pieces(k):
        prev, following, up, down = gathered[k]
        return [
            (texts, firsts[k], img_slot(0), None),
            (prev, 0, img_slot(3), None),
            (following, 0, img_slot(1), None),
            (up, 0, img_slot(2), upper),
            (down, 0, img_slot(2), lower),
        ]

    def over_img(col):
        col = log_add(col, lax.ppermute(col, "img", paired(4, 1)))
        return log_add(col, lax.ppermute(col, "img", paired(4, 2)))

    u0, texts0, row, col0 = logits_and_stats(whole_img, text_pieces(0), chunks[0], None)
    col0 = over_img(col0)
    u1, texts1, row, col1 = logits_and_stats(whole_img, text_pieces(1), chunks[1], row)
    for by in (1, 2, 4):
        row = log_add(row, swap(row, by))
    col1 = over_img(col1)

    targets = (positive - lax.axis_index("txt") * txt_rows).reshape(row.shape)
    text_slots = [img_slot(2), img_slot(1), img_slot(3), img_slot(0)]
    weights, picked, text_parts = [], [], []
    for k, (u, col) in enumerate(((u0, col0), (u1, col1))):
        w, pos, opposite, following, prev, own = weights_and_text_grad(
            u, whole_img, targets, row, col, firsts[k], text_slots
        )
        weights.append(w)
        picked.append(pos)
        from_below = lax.ppermute(opposite, "img", [(0, 1), (1, 2)])
        from_above = lax.ppermute(opposite, "img", [(3, 2), (2, 1)])
        from_prev = lax.ppermute(following + from_below, "img", up_ring)
        from_next = lax.ppermute(prev + from_above, "img", down_ring)
        text_parts.append(
            (own.astype(jnp.float32) + from_prev.astype(jnp.float32) + from_next.astype(jnp.float32)).astype(
                jnp.bfloat16
            )
        )
    text_grad = jnp.concatenate(text_parts, axis=0)
    loss = loss_terms(row, (col0, col1), picked, 4, 8)[None]
    for by in (1, 2, 4):
        loss += swap(loss, by)
    for by in (1, 2):
        loss += lax.ppermute(loss, "img", paired(4, by))
    mean_loss = loss[0] * (ln2 / (2.0 * txt_rows * 8))

    kept = [[txt_slot(0)], [txt_slot(2)], [txt_slot(4)], [txt_slot(6)]]
    sent = [txt_slot(flip) for flip in (1, 3, 5, 7)]
    sums = []
    eighth = width // 8
    for k in range(2):
        *own, other = image_grad_parts(weights, (texts0, texts1), k * image_half, image_half, kept + [sent])
        other = swap(other, 1)
        sums.append([own[j] + other[:, j * eighth : (j + 1) * eighth] for j in range(4)])
    (s0, x0, y0, d0), (s1, x1, y1, d1) = sums
    d0 = swap(d0, 2)
    d1 = swap(d1, 4)
    image_parts = []
    for s, x, y in ((s0, x0, y0 + d0), (s1, x1 + d1, y1)):
        x, y = swap(x, 2), swap(y, 4)
        image_parts.append(
            (s.astype(jnp.float32) + x.astype(jnp.float32) + y.astype(jnp.float32)).astype(jnp.bfloat16)
        )
    return mean_loss, jnp.concatenate(image_parts, axis=0), text_grad


def per_device(images, texts, positive):
    n_img, n_txt = lax.axis_size("img"), lax.axis_size("txt")
    if (n_img, n_txt) == (4, 8):
        return per_device_4x8(images, texts, positive)
    whole_img = lax.all_gather(images, "txt", axis=1, tiled=True)
    whole_txt = lax.all_gather(texts, "img", axis=1, tiled=True)
    img_rows = whole_img.shape[0]
    txt_rows = whole_txt.shape[0]
    sizes = chunk_rows(txt_rows)
    firsts = (0, sizes[0])

    def merged(part, axis):
        every = lax.all_gather(part, axis)
        top = jnp.max(every, axis=0)
        return top + jnp.log(jnp.sum(jnp.exp2(every - top), axis=0)) * log2e

    def first_slot():
        return jnp.int32(0)

    row, logits, chunks, cols = None, [], [], []
    for k in range(2):
        u, chunk, row, col = logits_and_stats(whole_img, [(whole_txt, firsts[k], first_slot, None)], sizes[k], row)
        logits.append(u)
        chunks.append(chunk)
        cols.append(merged(col, "img"))
    row = merged(row, "txt")
    targets = (positive - lax.axis_index("txt") * txt_rows).reshape(row.shape)
    weights, picked, text_parts = [], [], []
    for k in range(2):
        w, pos, part = weights_and_text_grad(logits[k], whole_img, targets, row, cols[k], firsts[k], [first_slot])
        weights.append(w)
        picked.append(pos)
        text_parts.append(part)
    (image_part,) = image_grad_parts(weights, chunks, 0, img_rows, [[first_slot]])
    loss = lax.psum(loss_terms(row, cols, picked, n_img, n_txt), ("img", "txt"))
    mean_loss = loss * (ln2 / (2.0 * txt_rows * n_txt))
    image_grad = lax.psum_scatter(image_part, "txt", scatter_dimension=1, tiled=True)
    text_grad = lax.psum_scatter(jnp.concatenate(text_parts, axis=0), "img", scatter_dimension=1, tiled=True)
    return mean_loss, image_grad, text_grad


def solution(mesh):
    placed = (P("img", "txt"), P("txt", "img"), P("img"))
    return jax.shard_map(
        per_device,
        mesh=mesh,
        in_specs=placed,
        out_specs=(P(), P("img", "txt"), P("txt", "img")),
        check_vma=False,
    )
```

```python
import functools
import math
import jax
import jax.numpy as jnp
from jax import lax
from jax.experimental import pallas as pl
from jax.experimental.pallas import tpu as pltpu
from jax.sharding import PartitionSpec as P

logit_scale = 100.0
log2e = math.log2(math.e)
ln2 = math.log(2.0)
strip = 32
vmem_bytes = 48 * 1024 * 1024

VMEM = pl.BlockSpec(memory_space=pltpu.VMEM)


def columns(slot, width):
    return pl.ds(pl.multiple_of(slot * width, width), width)


def in_hbm(array):
    return pltpu.with_memory_space_constraint(array, pltpu.HBM)


def params():
    return pltpu.CompilerParams(vmem_limit_bytes=vmem_bytes)


def cost(microseconds):
    return pl.CostEstimate(flops=int(1.1e9 * microseconds), bytes_accessed=1, transcendentals=0)


def log_add(*terms):
    larger = functools.reduce(jnp.maximum, terms)
    return larger + jnp.log(sum(jnp.exp2(term - larger) for term in terms)) * log2e


def lanes(x):
    return [x[:, k : k + 128] for k in range(0, x.shape[1], 128)]


def side_by_side(image_pieces, text_pieces, width):
    img_rows = image_pieces[0][0].shape[0]
    rows = text_pieces[0][0].shape[0]
    steps = 4
    bm, bt = img_rows // steps, rows // steps
    pieces = text_pieces + image_pieces

    def kernel(*refs):
        *sources, texts_ref, images_ref = refs
        texts_ref[...] = jnp.zeros(texts_ref.shape, jnp.bfloat16)
        for k, (source, (_, slot)) in enumerate(zip(sources, pieces)):
            target = texts_ref if k < len(text_pieces) else images_ref
            target[:, columns(slot(), source.shape[1])] = source[...]

    return pl.pallas_call(
        kernel,
        grid=(steps,),
        out_shape=(
            jax.ShapeDtypeStruct((rows, width), jnp.bfloat16),
            pltpu.HBM((img_rows, width), jnp.bfloat16),
        ),
        in_specs=[pl.BlockSpec((bt, piece.shape[1]), lambda i: (i, 0)) for piece, _ in text_pieces]
        + [pl.BlockSpec((bm, piece.shape[1]), lambda i: (i, 0)) for piece, _ in image_pieces],
        out_specs=(pl.BlockSpec((bt, width), lambda i: (i, 0)), pl.BlockSpec((bm, width), lambda i: (i, 0))),
        compiler_params=params(),
        cost_estimate=cost(10),
        name="side_by_side",
    )(*[in_hbm(piece) for piece, _ in pieces])


def logits_and_stats(images, texts, far, targets):
    img_rows, width = images.shape
    rows = texts.shape[0]
    steps, bm = targets.shape
    pieces = rows // 256
    some = bm // pieces

    def before(i):
        return jnp.maximum(i - 1, 0)

    def kernel(images_ref, texts_ref, targets_ref, *refs):
        if far is not None:
            one_ref, other_ref, *refs = refs
        u_ref, row_ref, col_ref, whole_ref, d_scr, rm_scr, rs_scr, cm_scr, cs_scr, target_scr, pos_scr = refs
        step = pl.program_id(0)

        @pl.when(step == 0)
        def _():
            cm_scr[...] = jnp.full(cm_scr.shape, -jnp.inf, jnp.float32)
            cs_scr[...] = jnp.zeros(cs_scr.shape, jnp.float32)
            pos_scr[...] = jnp.zeros(pos_scr.shape, jnp.float32)
            whole_ref[...] = texts_ref[...]
            if far is not None:
                whole_ref[:, columns(far[1](), one_ref.shape[1])] = jnp.where(far[2](), one_ref[...], other_ref[...])

        def matmul(j):
            at = slice(j * 256, (j + 1) * 256)
            d_scr[step % 2, :, at] = lax.dot_general(
                images_ref[...], whole_ref[at, :], (((1,), (1,)), ((), ())), preferred_element_type=jnp.float32
            )

        def elementwise(j):
            slot = (step + 1) % 2
            old = cm_scr[...]
            new = old
            ids = lax.broadcasted_iota(jnp.int32, (strip, 128), 1)
            picked = jnp.zeros((strip, 128), jnp.float32)
            for first in range(j * some, (j + 1) * some, strip):
                at = slice(first, first + strip)
                u = d_scr[slot, at, :] * (logit_scale * log2e)
                u_ref[at, :] = u
                target = target_scr[at, :] - ids
                for k, v in enumerate(lanes(u)):
                    picked = picked + jnp.where(target == 128 * k, v, 0.0)
                rm_scr[at, :] = functools.reduce(jnp.maximum, lanes(u))
                new = jnp.maximum(new, jnp.max(u.reshape(strip // 8, 8, rows), axis=0))
            pos_scr[...] += picked
            cm_scr[...] = new
            total = cs_scr[...] * jnp.exp2(old - new)
            for first in range(j * some, (j + 1) * some, strip):
                at = slice(first, first + strip)
                u = u_ref[at, :]
                row_max = rm_scr[at, :]
                rs_scr[at, :] = functools.reduce(jnp.add, [jnp.exp2(v - row_max) for v in lanes(u)])
                total = total + jnp.sum(jnp.exp2(u.reshape(strip // 8, 8, rows) - new[None]), axis=0)
            cs_scr[...] = total

        @pl.when(step > 0)
        def _():
            target_scr[...] = jnp.broadcast_to(targets_ref[pl.ds(step - 1, 1), :], (128, bm)).T

        @pl.when(step == 0)
        def _():
            for j in range(pieces):
                matmul(j)

        @pl.when(jnp.logical_and(step > 0, step < steps))
        def _():
            for j in range(pieces):
                matmul(j)
                elementwise(j)

        @pl.when(step == steps)
        def _():
            for j in range(pieces):
                elementwise(j)

        @pl.when(step > 0)
        def _():
            lane_max, lane_sum = rm_scr[...].T, rs_scr[...].T
            top = jnp.max(lane_max, axis=0, keepdims=True)
            row_sum = jnp.sum(lane_sum * jnp.exp2(lane_max - top), axis=0, keepdims=True)
            row_ref[pl.ds(step - 1, 1), :] = top + jnp.log(row_sum) * log2e

        @pl.when(step == steps)
        def _():
            top = jnp.max(cm_scr[...], axis=0, keepdims=True)
            col_sum = jnp.sum(cs_scr[...] * jnp.exp2(cm_scr[...] - top), axis=0, keepdims=True)
            col_ref[...] = top + jnp.log(col_sum) * log2e
            row_ref[pl.ds(steps, 1), :] = jnp.full((1, bm), jnp.sum(pos_scr[...]))

    return pl.pallas_call(
        kernel,
        grid=(steps + 1,),
        out_shape=(
            pltpu.HBM((img_rows, rows), jnp.float32),
            jax.ShapeDtypeStruct((steps + 1, bm), jnp.float32),
            jax.ShapeDtypeStruct((1, rows), jnp.float32),
            pltpu.HBM((rows, width), jnp.bfloat16),
        ),
        in_specs=[pl.BlockSpec((bm, width), lambda i: (jnp.minimum(i, steps - 1), 0)), VMEM, VMEM]
        + ([] if far is None else [VMEM, VMEM]),
        out_specs=(pl.BlockSpec((bm, rows), lambda i: (before(i), 0)), VMEM, VMEM, VMEM),
        scratch_shapes=[
            pltpu.VMEM((2, bm, rows), jnp.float32),
            pltpu.VMEM((bm, 128), jnp.float32),
            pltpu.VMEM((bm, 128), jnp.float32),
            pltpu.VMEM((8, rows), jnp.float32),
            pltpu.VMEM((8, rows), jnp.float32),
            pltpu.VMEM((bm, 128), jnp.int32),
            pltpu.VMEM((strip, 128), jnp.float32),
        ],
        compiler_params=params(),
        cost_estimate=cost(13),
        name="logits_and_stats",
    )(in_hbm(images), texts, targets, *(() if far is None else far[0]))


def weights_and_far(u, images, targets, row_lses, col_lses, slot, wide):
    img_rows = images.shape[0]
    rows = u.shape[1]
    steps, bm = targets.shape
    n_row, n_col = len(row_lses), len(col_lses)

    def now(i):
        return jnp.minimum(i, steps - 1)

    def before(i):
        return jnp.maximum(i - 1, 0)

    def kernel(u_ref, images_ref, targets_ref, *refs):
        row_refs, col_refs, refs = refs[:n_row], refs[n_row : n_row + n_col], refs[n_row + n_col :]
        w_ref, far_ref, loss_ref, w_scr, acc, row_ref, col_ref, row_scr, target_scr = refs
        step = pl.program_id(0)

        @pl.when(step == 0)
        def _():
            acc[...] = jnp.zeros(acc.shape, jnp.float32)
            row_ref[...] = log_add(*[ref[:steps, :] for ref in row_refs])
            col_ref[...] = log_add(*[ref[...] for ref in col_refs])
            picked = sum(ref[steps:, :1] for ref in row_refs)
            row_loss = jnp.sum(row_ref[...], keepdims=True) - 2.0 * picked
            col_loss = jnp.sum(col_ref[...], keepdims=True)
            lane = lax.broadcasted_iota(jnp.int32, (1, 128), 1)
            loss_ref[...] = jnp.where(lane == 0, row_loss, jnp.where(lane == 1, col_loss, 0.0))

        def elementwise():
            row_scr[...] = jnp.broadcast_to(row_ref[pl.ds(step, 1), :], (128, bm)).T
            target_scr[...] = jnp.broadcast_to(targets_ref[pl.ds(step, 1), :], (128, bm)).T
            ids = lax.broadcasted_iota(jnp.int32, (strip, 128), 1)
            col = col_ref[...]
            for first in range(0, bm, strip):
                at = slice(first, first + strip)
                row = row_scr[at, :]
                target = target_scr[at, :] - ids
                for k in range(0, rows, 128):
                    v = u_ref[at, k : k + 128]
                    weight = jnp.exp2(v - row) + jnp.exp2(v - col[:, k : k + 128]) - jnp.where(target == k, 2.0, 0.0)
                    weight = weight.astype(jnp.bfloat16)
                    w_ref[at, k : k + 128] = weight
                    w_scr[step % 2, at, k : k + 128] = weight

        def matmul():
            acc[...] += lax.dot_general(
                w_scr[(step + 1) % 2],
                images_ref[...],
                (((0,), (0,)), ((), ())),
                preferred_element_type=jnp.float32,
            )

        @pl.when(step == 0)
        def _():
            elementwise()

        @pl.when(jnp.logical_and(step > 0, step < steps))
        def _():
            elementwise()
            matmul()

        @pl.when(step == steps)
        def _():
            matmul()
            far_ref[...] = (logit_scale * acc[...]).astype(jnp.bfloat16)

    return pl.pallas_call(
        kernel,
        grid=(steps + 1,),
        out_shape=(
            pltpu.HBM((img_rows, rows), jnp.bfloat16),
            jax.ShapeDtypeStruct((rows, wide), jnp.bfloat16),
            jax.ShapeDtypeStruct((1, 128), jnp.float32),
        ),
        in_specs=[
            pl.BlockSpec((bm, rows), lambda i: (now(i), 0)),
            pl.BlockSpec((bm, wide), lambda i: (before(i), slot())),
        ]
        + [VMEM] * (1 + n_row + n_col),
        out_specs=(pl.BlockSpec((bm, rows), lambda i: (now(i), 0)), VMEM, VMEM),
        scratch_shapes=[
            pltpu.VMEM((2, bm, rows), jnp.bfloat16),
            pltpu.VMEM((rows, wide), jnp.float32),
            pltpu.VMEM((steps, bm), jnp.float32),
            pltpu.VMEM((1, rows), jnp.float32),
            pltpu.VMEM((bm, 128), jnp.float32),
            pltpu.VMEM((bm, 128), jnp.int32),
        ],
        compiler_params=params(),
        cost_estimate=cost(8),
        name="weights_and_far",
    )(in_hbm(u), in_hbm(images), targets, *row_lses, *col_lses)


def gradients(weights, images, texts, slots, text_wide, groups):
    img_rows, rows = weights.shape
    width = texts.shape[1]
    steps = 4
    bm = img_rows // steps
    wide = width // sum(len(group) for group in groups)
    n_text = len(slots)

    def kernel(w_ref, texts_ref, *refs):
        image_refs, text_outs, (*image_outs, acc, image_acc) = refs[:n_text], refs[n_text : 2 * n_text], refs[2 * n_text :]
        step = pl.program_id(0)

        @pl.when(step == 0)
        def _():
            acc[...] = jnp.zeros(acc.shape, jnp.float32)

        for k, image_ref in enumerate(image_refs):
            acc[k] += lax.dot_general(
                w_ref[...], image_ref[...], (((0,), (0,)), ((), ())), preferred_element_type=jnp.float32
            )
        image_acc[...] = logit_scale * jnp.dot(w_ref[...], texts_ref[...], preferred_element_type=jnp.float32)
        for out, group in zip(image_outs, groups):
            for k, slot in enumerate(group):
                out[:, k * wide : (k + 1) * wide] = image_acc[:, columns(slot(), wide)].astype(jnp.bfloat16)

        @pl.when(step == steps - 1)
        def _():
            for k, out in enumerate(text_outs):
                out[...] = (logit_scale * acc[k]).astype(jnp.bfloat16)

    def image_spec(slot):
        return pl.BlockSpec((bm, text_wide), lambda i: (i, slot()))

    return pl.pallas_call(
        kernel,
        grid=(steps,),
        out_shape=(jax.ShapeDtypeStruct((rows, text_wide), jnp.bfloat16),) * n_text
        + tuple(jax.ShapeDtypeStruct((img_rows, wide * len(group)), jnp.bfloat16) for group in groups),
        in_specs=[pl.BlockSpec((bm, rows), lambda i: (i, 0)), VMEM] + [image_spec(slot) for slot in slots],
        out_specs=(VMEM,) * n_text + tuple(pl.BlockSpec((bm, wide * len(g)), lambda i: (i, 0)) for g in groups),
        scratch_shapes=[
            pltpu.VMEM((n_text, rows, text_wide), jnp.float32),
            pltpu.VMEM((bm, width), jnp.float32),
        ],
        compiler_params=params(),
        cost_estimate=cost(18),
        name="gradients",
    )(in_hbm(weights), texts, *[in_hbm(images)] * n_text)


def together(*values):
    return lax.optimization_barrier(values)


def as_bf16_sum(*terms):
    return sum(term.astype(jnp.float32) for term in terms).astype(jnp.bfloat16)


def shifted(count, by):
    return [(i, (i + by) % count) for i in range(count)]


def paired(count, by):
    return [(i, i ^ by) for i in range(count)]


def per_device_4x8(images, texts, positive):
    img_rows = images.shape[0]
    txt_rows, quarter = texts.shape
    width = quarter * 4

    def swap(part, by):
        return lax.ppermute(part, "txt", paired(8, by))

    def over_z(part, by):
        return lax.ppermute(part, "img", paired(4, by))

    def across(part, by_z, by_txt):
        pairs = [(8 * z + c, 8 * (z ^ by_z) + (c ^ by_txt)) for z in range(4) for c in range(8)]
        return lax.ppermute(part, ("img", "txt"), pairs)

    def txt_slot(flip):
        return lambda: lax.axis_index("txt") ^ flip

    def img_slot(by):
        return lambda: lax.rem(lax.axis_index("img") + by, 4)

    targets = (positive - lax.axis_index("txt") * txt_rows).reshape(4, img_rows // 4)
    from_prev = lax.ppermute(texts, "img", shifted(4, 1))
    from_next = lax.ppermute(texts, "img", shifted(4, -1))
    parts = [images, swap(images, 2), swap(images, 4), swap(images, 6)]
    targets, from_prev, from_next, *parts = together(targets, from_prev, from_next, *parts)
    from_below = lax.ppermute(from_prev, "img", [(1, 2), (2, 3)])
    from_above = lax.ppermute(from_next, "img", [(1, 0), (2, 1)])
    parts += [swap(part, 1) for part in parts]
    image_pieces = [(part, txt_slot(flip)) for part, flip in zip(parts, (0, 2, 4, 6, 1, 3, 5, 7))]
    text_pieces = [(texts, img_slot(0)), (from_prev, img_slot(3)), (from_next, img_slot(1))]
    most_txt, whole_img = side_by_side(image_pieces, text_pieces, width)
    from_below, from_above, most_txt = together(from_below, from_above, most_txt)
    far = ((from_below, from_above), img_slot(2), lambda: lax.axis_index("img") >= 2)
    u, row, col, whole_txt = logits_and_stats(whole_img, most_txt, far, targets)

    other = swap(row, 1)
    last = lax.broadcasted_iota(jnp.int32, row.shape, 0) == 4
    row = jnp.where(last, row + other, log_add(row, other))
    rows = [row] + [swap(row, by) for by in (2, 4, 6)]
    cols = [col] + [over_z(col, by) for by in (1, 2, 3)]

    w, far_grad, loss = weights_and_far(u, whole_img, targets, rows, cols, img_slot(2), quarter)
    below = lax.ppermute(far_grad, "img", [(0, 1), (1, 2)])
    above = lax.ppermute(far_grad, "img", [(3, 2), (2, 1)])
    image_groups = [[txt_slot(flip)] for flip in (0, 2, 4, 6)] + [[txt_slot(flip) for flip in (1, 3, 5, 7)]]
    text_slots = [img_slot(1), img_slot(3), img_slot(0)]
    to_next, to_prev, own, *image_parts = gradients(w, whole_img, whole_txt, text_slots, quarter, image_groups)
    loss += across(loss, 1, 1)
    below, above, to_next, to_prev, *image_parts, loss = together(below, above, to_next, to_prev, *image_parts, loss)

    other = swap(image_parts.pop(), 1)
    eighth = width // 8
    s, x, y, d = [part + other[:, j * eighth : (j + 1) * eighth] for j, part in enumerate(image_parts)]
    losses = [across(loss, 2, 2), swap(loss, 4), swap(loss, 6)]
    to_next, to_prev = to_next + below, to_prev + above
    to_next, to_prev, s, x, y, d, *losses = together(to_next, to_prev, s, x, y, d, *losses)

    from_prev = lax.ppermute(to_next, "img", shifted(4, 1))
    from_next = lax.ppermute(to_prev, "img", shifted(4, -1))
    image_grad = as_bf16_sum(s, swap(x, 2), swap(y, 4), swap(d, 6))
    text_grad = as_bf16_sum(own, from_prev, from_next)
    loss = (loss + losses[0])[0, 0] + (loss + sum(losses))[0, 1]
    return loss * (ln2 / (2.0 * txt_rows * 8)), image_grad, text_grad


def per_device(images, texts, positive):
    n_img, n_txt = lax.axis_size("img"), lax.axis_size("txt")
    if (n_img, n_txt) == (4, 8):
        return per_device_4x8(images, texts, positive)

    def first_slot():
        return jnp.int32(0)

    def gathered(part, axis):
        every = lax.all_gather(part, axis)
        return [every[k] for k in range(lax.axis_size(axis))]

    whole_img = lax.all_gather(images, "txt", axis=1, tiled=True)
    whole_txt = lax.all_gather(texts, "img", axis=1, tiled=True)
    txt_rows, width = whole_txt.shape
    targets = (positive - lax.axis_index("txt") * txt_rows).reshape(4, whole_img.shape[0] // 4)
    u, row, col, whole_txt = logits_and_stats(whole_img, whole_txt, None, targets)
    rows, cols = gathered(row, "txt"), gathered(col, "img")
    w, _, loss = weights_and_far(u, whole_img, targets, rows, cols, first_slot, 256)
    text_part, image_part = gradients(w, whole_img, whole_txt, [first_slot], width, [[first_slot]])
    loss = lax.psum(loss[0, 0] / n_txt + loss[0, 1] / n_img, ("img", "txt"))
    mean_loss = loss * (ln2 / (2.0 * txt_rows * n_txt))
    image_grad = lax.psum_scatter(image_part, "txt", scatter_dimension=1, tiled=True)
    text_grad = lax.psum_scatter(text_part, "img", scatter_dimension=1, tiled=True)
    return mean_loss, image_grad, text_grad


def solution(mesh):
    placed = (P("img", "txt"), P("txt", "img"), P("img"))
    return jax.shard_map(
        per_device,
        mesh=mesh,
        in_specs=placed,
        out_specs=(P(), P("img", "txt"), P("txt", "img")),
        check_vma=False,
    )
```

```python
import functools
import math
import jax
import jax.numpy as jnp
from jax import lax
from jax.experimental import pallas as pl
from jax.experimental.pallas import tpu as pltpu
from jax.sharding import PartitionSpec as P

logit_scale = 100.0
log2e = math.log2(math.e)
ln2 = math.log(2.0)
strip = 32
vmem_bytes = 48 * 1024 * 1024

VMEM = pl.BlockSpec(memory_space=pltpu.VMEM)


def columns(slot, width):
    return pl.ds(pl.multiple_of(slot * width, width), width)


def in_hbm(array):
    return pltpu.with_memory_space_constraint(array, pltpu.HBM)


def params():
    return pltpu.CompilerParams(vmem_limit_bytes=vmem_bytes)


def cost(microseconds):
    return pl.CostEstimate(flops=int(1.1e9 * microseconds), bytes_accessed=1, transcendentals=0)


def log_add(*terms):
    larger = functools.reduce(jnp.maximum, terms)
    return larger + jnp.log(sum(jnp.exp2(term - larger) for term in terms)) * log2e


def lanes(x):
    return [x[:, k : k + 128] for k in range(0, x.shape[1], 128)]


def side_by_side(image_pieces, text_pieces, width):
    img_rows = image_pieces[0][0].shape[0]
    rows = text_pieces[0][0].shape[0]
    steps = 4
    bm, bt = img_rows // steps, rows // steps
    pieces = text_pieces + image_pieces

    def kernel(*refs):
        *sources, texts_ref, images_ref = refs
        texts_ref[...] = jnp.zeros(texts_ref.shape, jnp.bfloat16)
        for k, (source, (_, slot)) in enumerate(zip(sources, pieces)):
            target = texts_ref if k < len(text_pieces) else images_ref
            target[:, columns(slot(), source.shape[1])] = source[...]

    return pl.pallas_call(
        kernel,
        grid=(steps,),
        out_shape=(
            jax.ShapeDtypeStruct((rows, width), jnp.bfloat16),
            pltpu.HBM((img_rows, width), jnp.bfloat16),
        ),
        in_specs=[pl.BlockSpec((bt, piece.shape[1]), lambda i: (i, 0)) for piece, _ in text_pieces]
        + [pl.BlockSpec((bm, piece.shape[1]), lambda i: (i, 0)) for piece, _ in image_pieces],
        out_specs=(pl.BlockSpec((bt, width), lambda i: (i, 0)), pl.BlockSpec((bm, width), lambda i: (i, 0))),
        compiler_params=params(),
        cost_estimate=cost(0.01),
        name="side_by_side",
    )(*[in_hbm(piece) for piece, _ in pieces])


def logits_and_stats(images, texts, far, targets):
    img_rows, width = images.shape
    rows = texts.shape[0]
    steps, bm = targets.shape
    pieces = rows // 256
    some = bm // pieces

    def before(i):
        return jnp.maximum(i - 1, 0)

    def kernel(images_ref, texts_ref, targets_ref, *refs):
        if far is not None:
            one_ref, other_ref, *refs = refs
        u_ref, row_ref, col_ref, whole_ref, d_scr, rm_scr, rs_scr, cm_scr, cs_scr, target_scr, pos_scr = refs
        step = pl.program_id(0)

        @pl.when(step == 0)
        def _():
            cm_scr[...] = jnp.full(cm_scr.shape, -jnp.inf, jnp.float32)
            cs_scr[...] = jnp.zeros(cs_scr.shape, jnp.float32)
            pos_scr[...] = jnp.zeros(pos_scr.shape, jnp.float32)
            whole_ref[...] = texts_ref[...]
            if far is not None:
                whole_ref[:, columns(far[1](), one_ref.shape[1])] = jnp.where(far[2](), one_ref[...], other_ref[...])

        def matmul(j):
            at = slice(j * 256, (j + 1) * 256)
            d_scr[step % 2, :, at] = lax.dot_general(
                images_ref[...], whole_ref[at, :], (((1,), (1,)), ((), ())), preferred_element_type=jnp.float32
            )

        def elementwise(j):
            slot = (step + 1) % 2
            old = cm_scr[...]
            new = old
            ids = lax.broadcasted_iota(jnp.int32, (strip, 128), 1)
            picked = jnp.zeros((strip, 128), jnp.float32)
            for first in range(j * some, (j + 1) * some, strip):
                at = slice(first, first + strip)
                u = d_scr[slot, at, :] * (logit_scale * log2e)
                u_ref[at, :] = u
                target = target_scr[at, :] - ids
                found = jnp.zeros((strip, 128), jnp.float32)
                for k, v in enumerate(lanes(u)):
                    found = jnp.where(target == 128 * k, v, found)
                picked = picked + found
                rm_scr[at, :] = functools.reduce(jnp.maximum, lanes(u))
                new = jnp.maximum(new, jnp.max(u.reshape(strip // 8, 8, rows), axis=0))
            pos_scr[...] += picked
            cm_scr[...] = new
            total = cs_scr[...] * jnp.exp2(old - new)
            for first in range(j * some, (j + 1) * some, strip):
                at = slice(first, first + strip)
                u = u_ref[at, :]
                row_max = rm_scr[at, :]
                rs_scr[at, :] = functools.reduce(jnp.add, [jnp.exp2(v - row_max) for v in lanes(u)])
                total = total + jnp.sum(jnp.exp2(u.reshape(strip // 8, 8, rows) - new[None]), axis=0)
            cs_scr[...] = total

        @pl.when(step > 0)
        def _():
            target_scr[...] = jnp.broadcast_to(targets_ref[pl.ds(step - 1, 1), :], (128, bm)).T

        @pl.when(step == 0)
        def _():
            for j in range(pieces):
                matmul(j)

        @pl.when(jnp.logical_and(step > 0, step < steps))
        def _():
            for j in range(pieces):
                matmul(j)
                elementwise(j)

        @pl.when(step == steps)
        def _():
            for j in range(pieces):
                elementwise(j)

        @pl.when(step > 0)
        def _():
            lane_max, lane_sum = rm_scr[...].T, rs_scr[...].T
            top = jnp.max(lane_max, axis=0, keepdims=True)
            row_sum = jnp.sum(lane_sum * jnp.exp2(lane_max - top), axis=0, keepdims=True)
            row_ref[pl.ds(step - 1, 1), :] = top + jnp.log(row_sum) * log2e

        @pl.when(step == steps)
        def _():
            top = jnp.max(cm_scr[...], axis=0, keepdims=True)
            col_sum = jnp.sum(cs_scr[...] * jnp.exp2(cm_scr[...] - top), axis=0, keepdims=True)
            col_ref[...] = top + jnp.log(col_sum) * log2e
            row_ref[pl.ds(steps, 1), :] = jnp.full((1, bm), jnp.sum(pos_scr[...]))

    return pl.pallas_call(
        kernel,
        grid=(steps + 1,),
        out_shape=(
            pltpu.HBM((img_rows, rows), jnp.float32),
            jax.ShapeDtypeStruct((steps + 1, bm), jnp.float32),
            jax.ShapeDtypeStruct((1, rows), jnp.float32),
            pltpu.HBM((rows, width), jnp.bfloat16),
        ),
        in_specs=[pl.BlockSpec((bm, width), lambda i: (jnp.minimum(i, steps - 1), 0)), VMEM, VMEM]
        + ([] if far is None else [VMEM, VMEM]),
        out_specs=(pl.BlockSpec((bm, rows), lambda i: (before(i), 0)), VMEM, VMEM, VMEM),
        scratch_shapes=[
            pltpu.VMEM((2, bm, rows), jnp.float32),
            pltpu.VMEM((bm, 128), jnp.float32),
            pltpu.VMEM((bm, 128), jnp.float32),
            pltpu.VMEM((8, rows), jnp.float32),
            pltpu.VMEM((8, rows), jnp.float32),
            pltpu.VMEM((bm, 128), jnp.int32),
            pltpu.VMEM((strip, 128), jnp.float32),
        ],
        compiler_params=params(),
        cost_estimate=cost(13),
        name="logits_and_stats",
    )(in_hbm(images), texts, targets, *(() if far is None else far[0]))


def weights_and_far(u, images, targets, row_lses, col_lses, slot, wide, cuts):
    img_rows = images.shape[0]
    rows = u.shape[1]
    steps, bm = targets.shape
    n_row, n_col = len(row_lses), len(col_lses)

    def kernel(u_ref, images_ref, targets_ref, *refs):
        row_refs, col_refs, refs = refs[:n_row], refs[n_row : n_row + n_col], refs[n_row + n_col :]
        w_ref, loss_ref, *far_refs, acc, row_ref, col_ref, row_scr, target_scr = refs
        step = pl.program_id(0)

        @pl.when(step == 0)
        def _():
            acc[...] = jnp.zeros(acc.shape, jnp.float32)
            row_ref[...] = log_add(*[ref[:steps, :] for ref in row_refs])
            col_ref[...] = log_add(*[ref[...] for ref in col_refs])
            picked = sum(ref[steps:, :1] for ref in row_refs)
            row_loss = jnp.sum(row_ref[...], keepdims=True) - 2.0 * picked
            col_loss = jnp.sum(col_ref[...], keepdims=True)
            lane = lax.broadcasted_iota(jnp.int32, (1, 128), 1)
            loss_ref[...] = jnp.where(lane == 0, row_loss, jnp.where(lane == 1, col_loss, 0.0))

        row_scr[...] = jnp.broadcast_to(row_ref[pl.ds(step, 1), :], (128, bm)).T
        target_scr[...] = jnp.broadcast_to(targets_ref[pl.ds(step, 1), :], (128, bm)).T
        ids = lax.broadcasted_iota(jnp.int32, (strip, 128), 1)
        col = col_ref[...]
        for group in range(0, bm, 256):
            end = min(group + 256, bm)
            for first in range(group, end, strip):
                at = slice(first, first + strip)
                row = row_scr[at, :]
                target = target_scr[at, :] - ids
                for k in range(0, rows, 128):
                    v = u_ref[at, k : k + 128]
                    weight = jnp.exp2(v - row) + jnp.exp2(v - col[:, k : k + 128]) - jnp.where(target == k, 2.0, 0.0)
                    w_ref[at, k : k + 128] = weight.astype(jnp.bfloat16)
            acc[...] += lax.dot_general(
                w_ref[group:end, :],
                images_ref[group:end, :],
                (((0,), (0,)), ((), ())),
                preferred_element_type=jnp.float32,
            )

        @pl.when(step == steps - 1)
        def _():
            for far_ref, first, end in zip(far_refs, cuts, cuts[1:]):
                far_ref[...] = (logit_scale * acc[first:end, :]).astype(jnp.bfloat16)

    return pl.pallas_call(
        kernel,
        grid=(steps,),
        out_shape=(
            pltpu.HBM((img_rows, rows), jnp.bfloat16),
            jax.ShapeDtypeStruct((1, 128), jnp.float32),
        )
        + tuple(jax.ShapeDtypeStruct((end - first, wide), jnp.bfloat16) for first, end in zip(cuts, cuts[1:])),
        in_specs=[
            pl.BlockSpec((bm, rows), lambda i: (i, 0)),
            pl.BlockSpec((bm, wide), lambda i: (i, slot())),
        ]
        + [VMEM] * (1 + n_row + n_col),
        out_specs=(pl.BlockSpec((bm, rows), lambda i: (i, 0)), VMEM) + (VMEM,) * (len(cuts) - 1),
        scratch_shapes=[
            pltpu.VMEM((rows, wide), jnp.float32),
            pltpu.VMEM((steps, bm), jnp.float32),
            pltpu.VMEM((1, rows), jnp.float32),
            pltpu.VMEM((bm, 128), jnp.float32),
            pltpu.VMEM((bm, 128), jnp.int32),
        ],
        compiler_params=params(),
        cost_estimate=cost(8),
        name="weights_and_far",
    )(in_hbm(u), in_hbm(images), targets, *row_lses, *col_lses)


def gradients(weights, images, texts, slots, text_wide, groups, order, microseconds=10):
    img_rows, rows = weights.shape
    width = images.shape[1]
    steps = 4
    bm = img_rows // steps
    wide = width // max(1, sum(len(group) for group in groups))
    n_text = len(slots)

    def kernel(w_ref, _, *refs):
        if groups:
            texts_ref, *refs = refs
        image_refs, text_outs, (*image_outs, acc, image_acc) = refs[:n_text], refs[n_text : 2 * n_text], refs[2 * n_text :]
        step = pl.program_id(0)

        if slots:

            @pl.when(step == 0)
            def _():
                acc[...] = jnp.zeros(acc.shape, jnp.float32)

        for k, image_ref in enumerate(image_refs):
            acc[k] += lax.dot_general(
                w_ref[...], image_ref[...], (((0,), (0,)), ((), ())), preferred_element_type=jnp.float32
            )
        if groups:
            image_acc[...] = logit_scale * jnp.dot(w_ref[...], texts_ref[...], preferred_element_type=jnp.float32)
        for out, group in zip(image_outs, groups):
            for k, slot in enumerate(group):
                out[:, k * wide : (k + 1) * wide] = image_acc[:, columns(slot(), wide)].astype(jnp.bfloat16)

        @pl.when(step == steps - 1)
        def _():
            for k, out in enumerate(text_outs):
                out[...] = (logit_scale * acc[k]).astype(jnp.bfloat16)

    def image_spec(slot):
        return pl.BlockSpec((bm, text_wide), lambda i: (i, slot()))

    return pl.pallas_call(
        kernel,
        grid=(steps,),
        out_shape=(jax.ShapeDtypeStruct((rows, text_wide), jnp.bfloat16),) * n_text
        + tuple(jax.ShapeDtypeStruct((img_rows, wide * len(group)), jnp.bfloat16) for group in groups),
        in_specs=[pl.BlockSpec((bm, rows), lambda i: (i, 0)), VMEM] + [VMEM] * bool(groups) + [image_spec(slot) for slot in slots],
        out_specs=(VMEM,) * n_text + tuple(pl.BlockSpec((bm, wide * len(g)), lambda i: (i, 0)) for g in groups),
        scratch_shapes=[
            pltpu.VMEM((max(1, n_text), rows, text_wide), jnp.float32),
            pltpu.VMEM((bm, width), jnp.float32),
        ],
        compiler_params=params(),
        cost_estimate=cost(microseconds),
        name="gradients",
    )(in_hbm(weights), order, *([texts] if groups else []), *[in_hbm(images)] * n_text)


def together(*values):
    return lax.optimization_barrier(values)


def as_bf16_sum(*terms):
    return sum(term.astype(jnp.float32) for term in terms).astype(jnp.bfloat16)


def shifted(count, by):
    return [(i, (i + by) % count) for i in range(count)]


def paired(count, by):
    return [(i, i ^ by) for i in range(count)]


def per_device_4x8(images, texts, positive):
    img_rows = images.shape[0]
    txt_rows, quarter = texts.shape
    width = quarter * 4

    def swap(part, by):
        return lax.ppermute(part, "txt", paired(8, by))

    def over_z(part, by):
        return lax.ppermute(part, "img", paired(4, by))

    def across(part, by_z, by_txt):
        pairs = [(8 * z + c, 8 * (z ^ by_z) + (c ^ by_txt)) for z in range(4) for c in range(8)]
        return lax.ppermute(part, ("img", "txt"), pairs)

    def txt_slot(flip):
        return lambda: lax.axis_index("txt") ^ flip

    def img_slot(by):
        return lambda: lax.rem(lax.axis_index("img") + by, 4)

    targets = (positive - lax.axis_index("txt") * txt_rows).reshape(4, img_rows // 4)
    from_prev = lax.ppermute(texts, "img", shifted(4, 1))
    from_next = lax.ppermute(texts, "img", shifted(4, -1))
    parts = [images, swap(images, 2), swap(images, 4), swap(images, 6)]
    is_first = lax.axis_index("img") == 1
    from_middle = lax.ppermute(jnp.where(is_first, from_prev, from_next), "img", [(1, 2), (2, 1)])
    from_inner = lax.ppermute(jnp.where(is_first, from_next, from_prev), "img", [(1, 0), (2, 3)])
    parts += [swap(part, 1) for part in parts]
    image_pieces = [(part, txt_slot(flip)) for part, flip in zip(parts, (0, 2, 4, 6, 1, 3, 5, 7))]
    text_pieces = [(texts, img_slot(0)), (from_prev, img_slot(3)), (from_next, img_slot(1))]
    most_txt, whole_img = side_by_side(image_pieces, text_pieces, width)
    from_middle, from_inner, most_txt, whole_img = together(from_middle, from_inner, most_txt, whole_img)
    far = ((from_middle, from_inner), img_slot(2), lambda: lax.rem(lax.axis_index("img"), 3) > 0)
    u, row, col, whole_txt = logits_and_stats(whole_img, most_txt, far, targets)

    other = swap(row, 1)
    last = lax.broadcasted_iota(jnp.int32, row.shape, 0) == 4
    row = jnp.where(last, row + other, log_add(row, other))
    rows = [row] + [swap(row, by) for by in (2, 4, 6)]
    cols = [col] + [over_z(col, by) for by in (1, 2, 3)]

    w, loss, far_grad = weights_and_far(u, whole_img, targets, rows, cols, img_slot(2), quarter, (0, txt_rows))
    middle = lax.ppermute(far_grad, "img", [(1, 2), (2, 1)])
    outer = lax.ppermute(far_grad, "img", [(0, 1), (3, 2)])
    image_groups = [[txt_slot(flip)] for flip in (0, 2, 4, 6)] + [[txt_slot(flip) for flip in (1, 3, 5, 7)]]
    to_next, to_prev, *image_parts = gradients(
        w, whole_img, whole_txt, [img_slot(1), img_slot(3)], quarter, image_groups, row
    )
    loss += across(loss, 1, 1)
    middle, outer, to_next, to_prev, *image_parts, loss = together(
        middle, outer, to_next, to_prev, *image_parts, loss
    )

    other = swap(image_parts.pop(), 1)
    loss += across(loss, 2, 2)
    to_next += jnp.where(is_first, outer, middle)
    to_prev += jnp.where(is_first, middle, outer)
    eighth = width // 8
    s, x, y, d = [part + other[:, j * eighth : (j + 1) * eighth] for j, part in enumerate(image_parts)]
    to_next, to_prev, s, x, y, d, loss = together(to_next, to_prev, s, x, y, d, loss)

    from_prev = lax.ppermute(to_next, "img", shifted(4, 1))
    from_next = lax.ppermute(to_prev, "img", shifted(4, -1))
    own = gradients(w, whole_img, None, [img_slot(0)], quarter, [], loss, 0.01)[0]
    image_grad = as_bf16_sum(s, swap(x, 2), swap(y, 4), swap(d, 6))
    text_grad = as_bf16_sum(own, from_prev, from_next)
    loss = loss[0, 0] + (loss + swap(loss, 4))[0, 1]
    return loss * (ln2 / (2.0 * txt_rows * 8)), image_grad, text_grad


def per_device(images, texts, positive):
    n_img, n_txt = lax.axis_size("img"), lax.axis_size("txt")
    if (n_img, n_txt) == (4, 8):
        return per_device_4x8(images, texts, positive)

    def first_slot():
        return jnp.int32(0)

    def gathered(part, axis):
        every = lax.all_gather(part, axis)
        return [every[k] for k in range(lax.axis_size(axis))]

    whole_img = lax.all_gather(images, "txt", axis=1, tiled=True)
    whole_txt = lax.all_gather(texts, "img", axis=1, tiled=True)
    txt_rows, width = whole_txt.shape
    targets = (positive - lax.axis_index("txt") * txt_rows).reshape(4, whole_img.shape[0] // 4)
    u, row, col, whole_txt = logits_and_stats(whole_img, whole_txt, None, targets)
    rows, cols = gathered(row, "txt"), gathered(col, "img")
    w, loss, _ = weights_and_far(u, whole_img, targets, rows, cols, first_slot, 256, (0, txt_rows))
    text_part, image_part = gradients(w, whole_img, whole_txt, [first_slot], width, [[first_slot]], row)
    loss = lax.psum(loss[0, 0] / n_txt + loss[0, 1] / n_img, ("img", "txt"))
    mean_loss = loss * (ln2 / (2.0 * txt_rows * n_txt))
    image_grad = lax.psum_scatter(image_part, "txt", scatter_dimension=1, tiled=True)
    text_grad = lax.psum_scatter(text_part, "img", scatter_dimension=1, tiled=True)
    return mean_loss, image_grad, text_grad


def solution(mesh):
    placed = (P("img", "txt"), P("txt", "img"), P("img"))
    return jax.shard_map(
        per_device,
        mesh=mesh,
        in_specs=placed,
        out_specs=(P(), P("img", "txt"), P("txt", "img")),
        check_vma=False,
    )
```

```python
import functools
import math
import jax
import jax.numpy as jnp
from jax import lax
from jax.experimental import pallas as pl
from jax.experimental.pallas import tpu as pltpu
from jax.sharding import PartitionSpec as P

logit_scale = 100.0
log2e = math.log2(math.e)
ln2 = math.log(2.0)
strip = 32

VMEM = pl.BlockSpec(memory_space=pltpu.VMEM)


def columns(slot, width):
    return pl.ds(pl.multiple_of(slot * width, width), width)


def in_vmem(array):
    return pltpu.with_memory_space_constraint(array, pltpu.VMEM)


def block_of(step, size):
    return pl.ds(pl.multiple_of(step * size, size), size)


def params(mebibytes):
    return pltpu.CompilerParams(vmem_limit_bytes=mebibytes * 1024 * 1024)


def cost(microseconds):
    return pl.CostEstimate(flops=int(1.1e9 * microseconds), bytes_accessed=1, transcendentals=0)


def log_add(*terms):
    larger = functools.reduce(jnp.maximum, terms)
    return larger + jnp.log(sum(jnp.exp2(term - larger) for term in terms)) * log2e


def lanes(x):
    return [x[:, k : k + 128] for k in range(0, x.shape[1], 128)]


def merge_rows(row, other):
    def kernel(row_ref, other_ref, out_ref):
        row, other = row_ref[...], other_ref[...]
        last = lax.broadcasted_iota(jnp.int32, row.shape, 0) == row.shape[0] - 1
        out_ref[...] = jnp.where(last, row + other, log_add(row, other))

    return pl.pallas_call(
        kernel,
        out_shape=jax.ShapeDtypeStruct(row.shape, jnp.float32),
        in_specs=[VMEM, VMEM],
        out_specs=VMEM,
        compiler_params=params(4),
        cost_estimate=cost(0.5),
        name="merge_rows",
    )(row, other)


def side_by_side(image_pieces, text_pieces, width):
    img_rows = image_pieces[0][0].shape[0]
    rows = text_pieces[0][0].shape[0]
    steps = 4
    bm, bt = img_rows // steps, rows // steps
    pieces = text_pieces + image_pieces

    def kernel(*refs):
        *sources, texts_ref, images_ref = refs
        step = pl.program_id(0)
        texts_ref[block_of(step, bt), :] = jnp.zeros((bt, width), jnp.bfloat16)
        for k, (source, (_, slot)) in enumerate(zip(sources, pieces)):
            target, size = (texts_ref, bt) if k < len(text_pieces) else (images_ref, bm)
            target[block_of(step, size), columns(slot(), source.shape[1])] = source[...]

    return pl.pallas_call(
        kernel,
        grid=(steps,),
        out_shape=(pltpu.VMEM((rows, width), jnp.bfloat16), pltpu.VMEM((img_rows, width), jnp.bfloat16)),
        in_specs=[pl.BlockSpec((bt, piece.shape[1]), lambda i: (i, 0)) for piece, _ in text_pieces]
        + [pl.BlockSpec((bm, piece.shape[1]), lambda i: (i, 0)) for piece, _ in image_pieces],
        out_specs=(VMEM, VMEM),
        compiler_params=params(12),
        cost_estimate=cost(0.01),
        name="side_by_side",
    )(*[piece for piece, _ in pieces])


def logits_and_stats(images, texts, far, targets):
    img_rows, width = images.shape
    rows = texts.shape[0]
    steps, bm = targets.shape
    pieces = rows // 256
    some = bm // pieces

    def kernel(images_ref, texts_ref, targets_ref, *refs):
        if far is not None:
            one_ref, other_ref, *refs = refs
        u_ref, row_ref, col_ref, whole_ref, even_scr, odd_scr, rm_scr, rs_scr, cm_scr, cs_scr, target_scr, pos_scr = refs
        step = pl.program_id(0)

        @pl.when(step == 0)
        def _():
            cm_scr[...] = jnp.full(cm_scr.shape, -jnp.inf, jnp.float32)
            cs_scr[...] = jnp.zeros(cs_scr.shape, jnp.float32)
            pos_scr[...] = jnp.zeros(pos_scr.shape, jnp.float32)
            whole_ref[...] = texts_ref[...]
            if far is not None:
                whole_ref[:, columns(far[1](), one_ref.shape[1])] = jnp.where(far[2](), one_ref[...], other_ref[...])

        def matmul(j, d_scr):
            at = slice(j * 256, (j + 1) * 256)
            d_scr[:, at] = lax.dot_general(
                images_ref[block_of(step, bm), :], whole_ref[at, :], (((1,), (1,)), ((), ())), preferred_element_type=jnp.float32
            )

        def elementwise(j, d_scr):
            base = (step - 1) * bm
            old = cm_scr[...]
            new = old
            ids = lax.broadcasted_iota(jnp.int32, (strip, 128), 1)
            picked = jnp.zeros((strip, 128), jnp.float32)
            for first in range(j * some, (j + 1) * some, strip):
                at = slice(first, first + strip)
                here = pl.ds(pl.multiple_of(base + first, strip), strip)
                u = d_scr[at, :] * (logit_scale * log2e)
                u_ref[here, :] = u
                target = target_scr[at, :] - ids
                found = jnp.zeros((strip, 128), jnp.float32)
                for k, v in enumerate(lanes(u)):
                    found = jnp.where(target == 128 * k, v, found)
                picked = picked + found
                rm_scr[at, :] = functools.reduce(jnp.maximum, lanes(u))
                new = jnp.maximum(new, jnp.max(u.reshape(strip // 8, 8, rows), axis=0))
            pos_scr[...] += picked
            cm_scr[...] = new
            total = cs_scr[...] * jnp.exp2(old - new)
            for first in range(j * some, (j + 1) * some, strip):
                at = slice(first, first + strip)
                u = u_ref[pl.ds(pl.multiple_of(base + first, strip), strip), :]
                row_max = rm_scr[at, :]
                rs_scr[at, :] = functools.reduce(jnp.add, [jnp.exp2(v - row_max) for v in lanes(u)])
                total = total + jnp.sum(jnp.exp2(u.reshape(strip // 8, 8, rows) - new[None]), axis=0)
            cs_scr[...] = total

        @pl.when(step > 0)
        def _():
            target_scr[...] = jnp.broadcast_to(targets_ref[pl.ds(step - 1, 1), :], (128, bm)).T

        @pl.when(step == 0)
        def _():
            for j in range(pieces):
                matmul(j, even_scr)

        @pl.when(jnp.logical_and(step < steps, step % 2 == 1))
        def _():
            for j in range(pieces):
                matmul(j, odd_scr)
                elementwise(j, even_scr)

        @pl.when(jnp.logical_and(step > 0, jnp.logical_and(step < steps, step % 2 == 0)))
        def _():
            for j in range(pieces):
                matmul(j, even_scr)
                elementwise(j, odd_scr)

        @pl.when(step == steps)
        def _():
            for j in range(pieces):
                elementwise(j, odd_scr if steps % 2 == 0 else even_scr)

        @pl.when(step > 0)
        def _():
            lane_max, lane_sum = rm_scr[...].T, rs_scr[...].T
            top = jnp.max(lane_max, axis=0, keepdims=True)
            row_sum = jnp.sum(lane_sum * jnp.exp2(lane_max - top), axis=0, keepdims=True)
            row_ref[pl.ds(step - 1, 1), :] = top + jnp.log(row_sum) * log2e

        @pl.when(step == steps)
        def _():
            top = jnp.max(cm_scr[...], axis=0, keepdims=True)
            col_sum = jnp.sum(cs_scr[...] * jnp.exp2(cm_scr[...] - top), axis=0, keepdims=True)
            col_ref[...] = top + jnp.log(col_sum) * log2e
            row_ref[pl.ds(steps, 1), :] = jnp.full((1, bm), jnp.sum(pos_scr[...]))

    return pl.pallas_call(
        kernel,
        grid=(steps + 1,),
        out_shape=(
            pltpu.VMEM((img_rows, rows), jnp.float32),
            jax.ShapeDtypeStruct((steps + 1, bm), jnp.float32),
            jax.ShapeDtypeStruct((1, rows), jnp.float32),
            pltpu.VMEM((rows, width), jnp.bfloat16),
        ),
        in_specs=[VMEM] * (3 if far is None else 5),
        out_specs=(VMEM,) * 4,
        scratch_shapes=[
            pltpu.VMEM((bm, rows), jnp.float32),
            pltpu.VMEM((bm, rows), jnp.float32),
            pltpu.VMEM((bm, 128), jnp.float32),
            pltpu.VMEM((bm, 128), jnp.float32),
            pltpu.VMEM((8, rows), jnp.float32),
            pltpu.VMEM((8, rows), jnp.float32),
            pltpu.VMEM((bm, 128), jnp.int32),
            pltpu.VMEM((strip, 128), jnp.float32),
        ],
        compiler_params=params(12),
        cost_estimate=cost(13),
        name="logits_and_stats",
    )(in_vmem(images), in_vmem(texts), targets, *(() if far is None else far[0]))


def weights_and_far(u, images, targets, row_lses, col_lses, slot, wide, cuts):
    img_rows = images.shape[0]
    rows = u.shape[1]
    steps, bm = targets.shape
    n_row, n_col = len(row_lses), len(col_lses)
    groups = [(first, min(first + 256, bm)) for first in range(0, bm, 256)]

    def kernel(u_ref, images_ref, targets_ref, *refs):
        row_refs, col_refs, refs = refs[:n_row], refs[n_row : n_row + n_col], refs[n_row + n_col :]
        w_ref, loss_ref, *refs = refs
        far_refs, refs = refs[: len(cuts) - 1], refs[len(cuts) - 1 :]
        group_scrs, (acc, row_ref, col_ref, row_scr, target_scr) = refs[: len(groups)], refs[len(groups) :]
        step = pl.program_id(0)

        @pl.when(step == 0)
        def _():
            acc[...] = jnp.zeros(acc.shape, jnp.float32)
            row_ref[...] = log_add(*[ref[:steps, :] for ref in row_refs])
            col_ref[...] = log_add(*[ref[...] for ref in col_refs])
            picked = sum(ref[steps:, :1] for ref in row_refs)
            row_loss = jnp.sum(row_ref[...], keepdims=True) - 2.0 * picked
            col_loss = jnp.sum(col_ref[...], keepdims=True)
            lane = lax.broadcasted_iota(jnp.int32, (1, 128), 1)
            loss_ref[...] = jnp.where(lane == 0, row_loss, jnp.where(lane == 1, col_loss, 0.0))

        row_scr[...] = jnp.broadcast_to(row_ref[pl.ds(step, 1), :], (128, bm)).T
        target_scr[...] = jnp.broadcast_to(targets_ref[pl.ds(step, 1), :], (128, bm)).T
        ids = lax.broadcasted_iota(jnp.int32, (strip, 128), 1)
        col = col_ref[...]
        for (group, end), w_scr in zip(groups, group_scrs):
            rows_here = pl.ds(pl.multiple_of(step * bm + group, 128), end - group)
            for first in range(group, end, strip):
                at = slice(first, first + strip)
                here = pl.ds(pl.multiple_of(step * bm + first, strip), strip)
                row = row_scr[at, :]
                target = target_scr[at, :] - ids
                for k in range(0, rows, 128):
                    v = u_ref[here, k : k + 128]
                    weight = jnp.exp2(v - row) + jnp.exp2(v - col[:, k : k + 128]) - jnp.where(target == k, 2.0, 0.0)
                    weight = weight.astype(jnp.bfloat16)
                    w_ref[here, k : k + 128] = weight
                    w_scr[first - group : first - group + strip, k : k + 128] = weight
            acc[...] += lax.dot_general(
                w_scr[...],
                images_ref[rows_here, columns(slot(), wide)],
                (((0,), (0,)), ((), ())),
                preferred_element_type=jnp.float32,
            )

        @pl.when(step == steps - 1)
        def _():
            for far_ref, first, end in zip(far_refs, cuts, cuts[1:]):
                far_ref[...] = (logit_scale * acc[first:end, :]).astype(jnp.bfloat16)

    return pl.pallas_call(
        kernel,
        grid=(steps,),
        out_shape=(
            pltpu.VMEM((img_rows, rows), jnp.bfloat16),
            jax.ShapeDtypeStruct((1, 128), jnp.float32),
        )
        + tuple(jax.ShapeDtypeStruct((end - first, wide), jnp.bfloat16) for first, end in zip(cuts, cuts[1:])),
        in_specs=[VMEM] * (3 + n_row + n_col),
        out_specs=(VMEM,) * (len(cuts) + 1),
        scratch_shapes=[pltpu.VMEM((end - first, rows), jnp.bfloat16) for first, end in groups]
        + [
            pltpu.VMEM((rows, wide), jnp.float32),
            pltpu.VMEM((steps, bm), jnp.float32),
            pltpu.VMEM((1, rows), jnp.float32),
            pltpu.VMEM((bm, 128), jnp.float32),
            pltpu.VMEM((bm, 128), jnp.int32),
        ],
        compiler_params=params(8),
        cost_estimate=cost(8),
        name="weights_and_far",
    )(in_vmem(u), in_vmem(images), targets, *row_lses, *col_lses)


def gradients(weights, images, texts, slots, text_wide, groups, order, microseconds=10):
    img_rows, rows = weights.shape
    width = images.shape[1]
    steps = 4
    bm = img_rows // steps
    wide = width // max(1, sum(len(group) for group in groups))
    n_text = len(slots)

    def kernel(w_ref, _, *refs):
        if groups:
            texts_ref, *refs = refs
        if slots:
            images_ref, *refs = refs
        text_outs, (*image_outs, acc, image_acc) = refs[:n_text], refs[n_text:]
        step = pl.program_id(0)
        here = block_of(step, bm)

        if slots:

            @pl.when(step == 0)
            def _():
                acc[...] = jnp.zeros(acc.shape, jnp.float32)

        for k, slot in enumerate(slots):
            acc[k] += lax.dot_general(
                w_ref[here, :],
                images_ref[here, columns(slot(), text_wide)],
                (((0,), (0,)), ((), ())),
                preferred_element_type=jnp.float32,
            )
        if groups:
            image_acc[...] = logit_scale * jnp.dot(
                w_ref[here, :], texts_ref[...], preferred_element_type=jnp.float32
            )
        for out, group in zip(image_outs, groups):
            for k, slot in enumerate(group):
                out[:, k * wide : (k + 1) * wide] = image_acc[:, columns(slot(), wide)].astype(jnp.bfloat16)

        @pl.when(step == steps - 1)
        def _():
            for k, out in enumerate(text_outs):
                out[...] = (logit_scale * acc[k]).astype(jnp.bfloat16)

    return pl.pallas_call(
        kernel,
        grid=(steps,),
        out_shape=(jax.ShapeDtypeStruct((rows, text_wide), jnp.bfloat16),) * n_text
        + tuple(jax.ShapeDtypeStruct((img_rows, wide * len(group)), jnp.bfloat16) for group in groups),
        in_specs=[VMEM] * (2 + bool(groups) + bool(slots)),
        out_specs=(VMEM,) * n_text + tuple(pl.BlockSpec((bm, wide * len(g)), lambda i: (i, 0)) for g in groups),
        scratch_shapes=[
            pltpu.VMEM((max(1, n_text), rows, text_wide), jnp.float32),
            pltpu.VMEM((bm, width), jnp.float32),
        ],
        compiler_params=params(14),
        cost_estimate=cost(microseconds),
        name="gradients",
    )(in_vmem(weights), order, *([in_vmem(texts)] if groups else []), *([in_vmem(images)] if slots else []))


def together(*values):
    return lax.optimization_barrier(values)


def as_bf16_sum(*terms):
    return sum(term.astype(jnp.float32) for term in terms).astype(jnp.bfloat16)


def shifted(count, by):
    return [(i, (i + by) % count) for i in range(count)]


def paired(count, by):
    return [(i, i ^ by) for i in range(count)]


def per_device_4x8(images, texts, positive):
    img_rows = images.shape[0]
    txt_rows, quarter = texts.shape
    width = quarter * 4

    def swap(part, by):
        return lax.ppermute(part, "txt", paired(8, by))

    def over_z(part, by):
        return lax.ppermute(part, "img", paired(4, by))

    def across(part, by_z, by_txt):
        pairs = [(8 * z + c, 8 * (z ^ by_z) + (c ^ by_txt)) for z in range(4) for c in range(8)]
        return lax.ppermute(part, ("img", "txt"), pairs)

    def txt_slot(flip):
        return lambda: lax.axis_index("txt") ^ flip

    def img_slot(by):
        return lambda: lax.rem(lax.axis_index("img") + by, 4)

    targets = (positive - lax.axis_index("txt") * txt_rows).reshape(4, img_rows // 4)
    from_prev = lax.ppermute(texts, "img", shifted(4, 1))
    from_next = lax.ppermute(texts, "img", shifted(4, -1))
    parts = [images, swap(images, 2), swap(images, 4), swap(images, 6)]
    is_first = lax.axis_index("img") == 1
    from_middle = lax.ppermute(jnp.where(is_first, from_prev, from_next), "img", [(1, 2), (2, 1)])
    from_inner = lax.ppermute(jnp.where(is_first, from_next, from_prev), "img", [(1, 0), (2, 3)])
    parts += [swap(part, 1) for part in parts]
    image_pieces = [(part, txt_slot(flip)) for part, flip in zip(parts, (0, 2, 4, 6, 1, 3, 5, 7))]
    text_pieces = [(texts, img_slot(0)), (from_prev, img_slot(3)), (from_next, img_slot(1))]
    most_txt, whole_img = side_by_side(image_pieces, text_pieces, width)
    from_middle, from_inner, most_txt, whole_img = together(from_middle, from_inner, most_txt, whole_img)
    far = ((from_middle, from_inner), img_slot(2), lambda: lax.rem(lax.axis_index("img"), 3) > 0)
    u, row, col, whole_txt = logits_and_stats(whole_img, most_txt, far, targets)

    row = merge_rows(row, swap(row, 1))
    rows = [row] + [swap(row, by) for by in (2, 4, 6)]
    cols = [col] + [over_z(col, by) for by in (1, 2, 3)]

    w, loss, far_grad = weights_and_far(u, whole_img, targets, rows, cols, img_slot(2), quarter, (0, txt_rows))
    middle = lax.ppermute(far_grad, "img", [(1, 2), (2, 1)])
    outer = lax.ppermute(far_grad, "img", [(0, 1), (3, 2)])
    image_groups = [[txt_slot(flip)] for flip in (0, 2, 4, 6)] + [[txt_slot(flip) for flip in (1, 3, 5, 7)]]
    to_next, to_prev, *image_parts = gradients(
        w, whole_img, whole_txt, [img_slot(1), img_slot(3)], quarter, image_groups, row
    )
    loss += across(loss, 1, 1)
    middle, outer, to_next, to_prev, *image_parts, loss = together(
        middle, outer, to_next, to_prev, *image_parts, loss
    )

    other = swap(image_parts.pop(), 1)
    loss += across(loss, 2, 2)
    to_next += jnp.where(is_first, outer, middle)
    to_prev += jnp.where(is_first, middle, outer)
    eighth = width // 8
    s, x, y, d = [part + other[:, j * eighth : (j + 1) * eighth] for j, part in enumerate(image_parts)]
    to_next, to_prev, s, x, y, d, loss = together(to_next, to_prev, s, x, y, d, loss)

    from_prev = lax.ppermute(to_next, "img", shifted(4, 1))
    from_next = lax.ppermute(to_prev, "img", shifted(4, -1))
    own = gradients(w, whole_img, None, [img_slot(0)], quarter, [], loss, 0.01)[0]
    image_grad = as_bf16_sum(s, swap(x, 2), swap(y, 4), swap(d, 6))
    text_grad = as_bf16_sum(own, from_prev, from_next)
    loss = loss[0, 0] + (loss + swap(loss, 4))[0, 1]
    return loss * (ln2 / (2.0 * txt_rows * 8)), image_grad, text_grad


def per_device(images, texts, positive):
    n_img, n_txt = lax.axis_size("img"), lax.axis_size("txt")
    if (n_img, n_txt) == (4, 8):
        return per_device_4x8(images, texts, positive)

    def first_slot():
        return jnp.int32(0)

    def gathered(part, axis):
        every = lax.all_gather(part, axis)
        return [every[k] for k in range(lax.axis_size(axis))]

    whole_img = lax.all_gather(images, "txt", axis=1, tiled=True)
    whole_txt = lax.all_gather(texts, "img", axis=1, tiled=True)
    txt_rows, width = whole_txt.shape
    targets = (positive - lax.axis_index("txt") * txt_rows).reshape(4, whole_img.shape[0] // 4)
    u, row, col, whole_txt = logits_and_stats(whole_img, whole_txt, None, targets)
    rows, cols = gathered(row, "txt"), gathered(col, "img")
    w, loss, _ = weights_and_far(u, whole_img, targets, rows, cols, first_slot, 256, (0, txt_rows))
    text_part, image_part = gradients(w, whole_img, whole_txt, [first_slot], width, [[first_slot]], row)
    loss = lax.psum(loss[0, 0] / n_txt + loss[0, 1] / n_img, ("img", "txt"))
    mean_loss = loss * (ln2 / (2.0 * txt_rows * n_txt))
    image_grad = lax.psum_scatter(image_part, "txt", scatter_dimension=1, tiled=True)
    text_grad = lax.psum_scatter(text_part, "img", scatter_dimension=1, tiled=True)
    return mean_loss, image_grad, text_grad


def solution(mesh):
    placed = (P("img", "txt"), P("txt", "img"), P("img"))
    return jax.shard_map(
        per_device,
        mesh=mesh,
        in_specs=placed,
        out_specs=(P(), P("img", "txt"), P("txt", "img")),
        check_vma=False,
    )
```

```python
import functools
import math
import jax
import jax.numpy as jnp
from jax import lax
from jax.experimental import pallas as pl
from jax.experimental.pallas import tpu as pltpu
from jax.sharding import PartitionSpec as P

logit_scale = 100.0
log2e = math.log2(math.e)
ln2 = math.log(2.0)
strip = 32

VMEM = pl.BlockSpec(memory_space=pltpu.VMEM)


def columns(slot, width):
    return pl.ds(pl.multiple_of(slot * width, width), width)


def in_vmem(array):
    return pltpu.with_memory_space_constraint(array, pltpu.VMEM)


def block_of(step, size):
    return pl.ds(pl.multiple_of(step * size, size), size)


def params(mebibytes):
    return pltpu.CompilerParams(vmem_limit_bytes=mebibytes * 1024 * 1024)


def cost(microseconds):
    return pl.CostEstimate(flops=int(1.1e9 * microseconds), bytes_accessed=1, transcendentals=0)


def log_add(*terms):
    larger = functools.reduce(jnp.maximum, terms)
    return larger + jnp.log(sum(jnp.exp2(term - larger) for term in terms)) * log2e


def lanes(x):
    return [x[:, k : k + 128] for k in range(0, x.shape[1], 128)]


def merge_rows(row, other):
    def kernel(row_ref, other_ref, out_ref):
        row, other = row_ref[...], other_ref[...]
        last = lax.broadcasted_iota(jnp.int32, row.shape, 0) == row.shape[0] - 1
        out_ref[...] = jnp.where(last, row + other, log_add(row, other))

    return pl.pallas_call(
        kernel,
        out_shape=jax.ShapeDtypeStruct(row.shape, jnp.float32),
        in_specs=[VMEM, VMEM],
        out_specs=VMEM,
        compiler_params=params(4),
        cost_estimate=cost(0.5),
        name="merge_rows",
    )(row, other)


def side_by_side(image_pieces, text_pieces, width, targets):
    img_rows = image_pieces[0][0].shape[0]
    rows = text_pieces[0][0].shape[0]
    steps = 4
    bm, bt = img_rows // steps, rows // steps
    pieces = text_pieces + image_pieces

    def kernel(*refs):
        *sources, targets_ref, texts_ref, images_ref, spread_ref = refs
        step = pl.program_id(0)
        spread_ref[block_of(step, bm), :] = jnp.broadcast_to(targets_ref[pl.ds(step, 1), :], (128, bm)).T
        texts_ref[block_of(step, bt), :] = jnp.zeros((bt, width), jnp.bfloat16)
        for k, (source, (_, slot)) in enumerate(zip(sources, pieces)):
            target, size = (texts_ref, bt) if k < len(text_pieces) else (images_ref, bm)
            target[block_of(step, size), columns(slot(), source.shape[1])] = source[...]

    return pl.pallas_call(
        kernel,
        grid=(steps,),
        out_shape=(
            pltpu.VMEM((rows, width), jnp.bfloat16),
            pltpu.VMEM((img_rows, width), jnp.bfloat16),
            pltpu.VMEM((img_rows, 128), jnp.int32),
        ),
        in_specs=[pl.BlockSpec((bt, piece.shape[1]), lambda i: (i, 0)) for piece, _ in text_pieces]
        + [pl.BlockSpec((bm, piece.shape[1]), lambda i: (i, 0)) for piece, _ in image_pieces]
        + [VMEM],
        out_specs=(VMEM, VMEM, VMEM),
        compiler_params=params(12),
        cost_estimate=cost(0.01),
        name="side_by_side",
    )(*[piece for piece, _ in pieces], targets)


def logits_and_stats(images, texts, far, targets):
    img_rows, width = images.shape
    rows = texts.shape[0]
    steps = 4
    bm = img_rows // steps
    pieces = rows // 256
    some = bm // pieces

    def kernel(images_ref, texts_ref, targets_ref, *refs):
        if far is not None:
            one_ref, other_ref, *refs = refs
        u_ref, row_ref, col_ref, whole_ref, even_scr, odd_scr, rm_scr, rs_scr, cm_scr, cs_scr, pos_scr = refs
        step = pl.program_id(0)

        @pl.when(step == 0)
        def _():
            cm_scr[...] = jnp.full(cm_scr.shape, -jnp.inf, jnp.float32)
            cs_scr[...] = jnp.zeros(cs_scr.shape, jnp.float32)
            pos_scr[...] = jnp.zeros(pos_scr.shape, jnp.float32)
            whole_ref[...] = texts_ref[...]
            if far is not None:
                whole_ref[:, columns(far[1](), one_ref.shape[1])] = jnp.where(far[2](), one_ref[...], other_ref[...])

        def matmul(j, d_scr):
            at = slice(j * 256, (j + 1) * 256)
            d_scr[:, at] = lax.dot_general(
                images_ref[block_of(step, bm), :], whole_ref[at, :], (((1,), (1,)), ((), ())), preferred_element_type=jnp.float32
            )

        def elementwise(j, d_scr):
            base = (step - 1) * bm
            old = cm_scr[...]
            new = old
            ids = lax.broadcasted_iota(jnp.int32, (strip, 128), 1)
            picked = jnp.zeros((strip, 128), jnp.float32)
            for first in range(j * some, (j + 1) * some, strip):
                at = slice(first, first + strip)
                here = pl.ds(pl.multiple_of(base + first, strip), strip)
                u = d_scr[at, :] * (logit_scale * log2e)
                u_ref[here, :] = u
                target = targets_ref[here, :] - ids
                found = jnp.zeros((strip, 128), jnp.float32)
                for k, v in enumerate(lanes(u)):
                    found = jnp.where(target == 128 * k, v, found)
                picked = picked + found
                rm_scr[at, :] = functools.reduce(jnp.maximum, lanes(u))
                new = jnp.maximum(new, jnp.max(u.reshape(strip // 8, 8, rows), axis=0))
            pos_scr[...] += picked
            cm_scr[...] = new
            total = cs_scr[...] * jnp.exp2(old - new)
            for first in range(j * some, (j + 1) * some, strip):
                at = slice(first, first + strip)
                u = u_ref[pl.ds(pl.multiple_of(base + first, strip), strip), :]
                row_max = rm_scr[at, :]
                rs_scr[at, :] = functools.reduce(jnp.add, [jnp.exp2(v - row_max) for v in lanes(u)])
                total = total + jnp.sum(jnp.exp2(u.reshape(strip // 8, 8, rows) - new[None]), axis=0)
            cs_scr[...] = total

        @pl.when(step == 0)
        def _():
            for j in range(pieces):
                matmul(j, even_scr)

        @pl.when(jnp.logical_and(step < steps, step % 2 == 1))
        def _():
            for j in range(pieces):
                matmul(j, odd_scr)
                elementwise(j, even_scr)

        @pl.when(jnp.logical_and(step > 0, jnp.logical_and(step < steps, step % 2 == 0)))
        def _():
            for j in range(pieces):
                matmul(j, even_scr)
                elementwise(j, odd_scr)

        @pl.when(step == steps)
        def _():
            for j in range(pieces):
                elementwise(j, odd_scr if steps % 2 == 0 else even_scr)

        @pl.when(step > 0)
        def _():
            lane_max, lane_sum = rm_scr[...].T, rs_scr[...].T
            top = jnp.max(lane_max, axis=0, keepdims=True)
            row_sum = jnp.sum(lane_sum * jnp.exp2(lane_max - top), axis=0, keepdims=True)
            row_ref[pl.ds(step - 1, 1), :] = top + jnp.log(row_sum) * log2e

        @pl.when(step == steps)
        def _():
            top = jnp.max(cm_scr[...], axis=0, keepdims=True)
            col_sum = jnp.sum(cs_scr[...] * jnp.exp2(cm_scr[...] - top), axis=0, keepdims=True)
            col_ref[...] = top + jnp.log(col_sum) * log2e
            row_ref[pl.ds(steps, 1), :] = jnp.full((1, bm), jnp.sum(pos_scr[...]))

    return pl.pallas_call(
        kernel,
        grid=(steps + 1,),
        out_shape=(
            pltpu.VMEM((img_rows, rows), jnp.float32),
            jax.ShapeDtypeStruct((steps + 1, bm), jnp.float32),
            jax.ShapeDtypeStruct((1, rows), jnp.float32),
            pltpu.VMEM((rows, width), jnp.bfloat16),
        ),
        in_specs=[VMEM] * (3 if far is None else 5),
        out_specs=(VMEM,) * 4,
        scratch_shapes=[
            pltpu.VMEM((bm, rows), jnp.float32),
            pltpu.VMEM((bm, rows), jnp.float32),
            pltpu.VMEM((bm, 128), jnp.float32),
            pltpu.VMEM((bm, 128), jnp.float32),
            pltpu.VMEM((8, rows), jnp.float32),
            pltpu.VMEM((8, rows), jnp.float32),
            pltpu.VMEM((strip, 128), jnp.float32),
        ],
        compiler_params=params(12),
        cost_estimate=cost(13),
        name="logits_and_stats",
    )(in_vmem(images), in_vmem(texts), in_vmem(targets), *(() if far is None else map(in_vmem, far[0])))


def weights_and_far(u, images, targets, row_lses, col_lses, slot, wide, cuts):
    img_rows = images.shape[0]
    rows = u.shape[1]
    steps = 4
    bm = img_rows // steps
    n_row, n_col = len(row_lses), len(col_lses)
    groups = [(first, min(first + 256, bm)) for first in range(0, bm, 256)]

    def kernel(u_ref, images_ref, targets_ref, *refs):
        row_refs, col_refs, refs = refs[:n_row], refs[n_row : n_row + n_col], refs[n_row + n_col :]
        w_ref, loss_ref, *refs = refs
        far_refs, refs = refs[: len(cuts) - 1], refs[len(cuts) - 1 :]
        group_scrs, (acc, row_ref, col_ref, row_scr) = refs[: len(groups)], refs[len(groups) :]
        step = pl.program_id(0)

        @pl.when(step == 0)
        def _():
            acc[...] = jnp.zeros(acc.shape, jnp.float32)
            row_ref[...] = log_add(*[ref[:steps, :] for ref in row_refs])
            col_ref[...] = log_add(*[ref[...] for ref in col_refs])
            picked = sum(ref[steps:, :1] for ref in row_refs)
            row_loss = jnp.sum(row_ref[...], keepdims=True) - 2.0 * picked
            col_loss = jnp.sum(col_ref[...], keepdims=True)
            lane = lax.broadcasted_iota(jnp.int32, (1, 128), 1)
            loss_ref[...] = jnp.where(lane == 0, row_loss, jnp.where(lane == 1, col_loss, 0.0))

        row_scr[...] = jnp.broadcast_to(row_ref[pl.ds(step, 1), :], (128, bm)).T
        ids = lax.broadcasted_iota(jnp.int32, (strip, 128), 1)
        col = col_ref[...]
        for (group, end), w_scr in zip(groups, group_scrs):
            rows_here = pl.ds(pl.multiple_of(step * bm + group, 128), end - group)
            for first in range(group, end, strip):
                at = slice(first, first + strip)
                here = pl.ds(pl.multiple_of(step * bm + first, strip), strip)
                row = row_scr[at, :]
                target = targets_ref[here, :] - ids
                for k in range(0, rows, 128):
                    v = u_ref[here, k : k + 128]
                    weight = jnp.exp2(v - row) + jnp.exp2(v - col[:, k : k + 128]) - jnp.where(target == k, 2.0, 0.0)
                    weight = weight.astype(jnp.bfloat16)
                    w_ref[here, k : k + 128] = weight
                    w_scr[first - group : first - group + strip, k : k + 128] = weight
            acc[...] += lax.dot_general(
                w_scr[...],
                images_ref[rows_here, columns(slot(), wide)],
                (((0,), (0,)), ((), ())),
                preferred_element_type=jnp.float32,
            )

        @pl.when(step == steps - 1)
        def _():
            for far_ref, first, end in zip(far_refs, cuts, cuts[1:]):
                far_ref[...] = (logit_scale * acc[first:end, :]).astype(jnp.bfloat16)

    return pl.pallas_call(
        kernel,
        grid=(steps,),
        out_shape=(
            pltpu.VMEM((img_rows, rows), jnp.bfloat16),
            jax.ShapeDtypeStruct((1, 128), jnp.float32),
        )
        + tuple(pltpu.VMEM((end - first, wide), jnp.bfloat16) for first, end in zip(cuts, cuts[1:])),
        in_specs=[VMEM] * (3 + n_row + n_col),
        out_specs=(VMEM,) * (len(cuts) + 1),
        scratch_shapes=[pltpu.VMEM((end - first, rows), jnp.bfloat16) for first, end in groups]
        + [
            pltpu.VMEM((rows, wide), jnp.float32),
            pltpu.VMEM((steps, bm), jnp.float32),
            pltpu.VMEM((1, rows), jnp.float32),
            pltpu.VMEM((bm, 128), jnp.float32),
        ],
        compiler_params=params(8),
        cost_estimate=cost(8),
        name="weights_and_far",
    )(in_vmem(u), in_vmem(images), in_vmem(targets), *map(in_vmem, row_lses), *map(in_vmem, col_lses))


def gradients(weights, images, texts, slots, text_wide, groups, order, microseconds=10):
    img_rows, rows = weights.shape
    width = images.shape[1]
    steps = 4
    bm = img_rows // steps
    wide = width // max(1, sum(len(group) for group in groups))
    n_text = len(slots)

    def kernel(w_ref, _, *refs):
        if groups:
            texts_ref, *refs = refs
        if slots:
            images_ref, *refs = refs
        text_outs, (*image_outs, acc, image_acc) = refs[:n_text], refs[n_text:]
        step = pl.program_id(0)
        here = block_of(step, bm)

        if slots:

            @pl.when(step == 0)
            def _():
                acc[...] = jnp.zeros(acc.shape, jnp.float32)

        for k, slot in enumerate(slots):
            acc[k] += lax.dot_general(
                w_ref[here, :],
                images_ref[here, columns(slot(), text_wide)],
                (((0,), (0,)), ((), ())),
                preferred_element_type=jnp.float32,
            )
        if groups:
            image_acc[...] = logit_scale * jnp.dot(
                w_ref[here, :], texts_ref[...], preferred_element_type=jnp.float32
            )
        for out, group in zip(image_outs, groups):
            for k, slot in enumerate(group):
                out[here, k * wide : (k + 1) * wide] = image_acc[:, columns(slot(), wide)].astype(jnp.bfloat16)

        @pl.when(step == steps - 1)
        def _():
            for k, out in enumerate(text_outs):
                out[...] = (logit_scale * acc[k]).astype(jnp.bfloat16)

    return pl.pallas_call(
        kernel,
        grid=(steps,),
        out_shape=(pltpu.VMEM((rows, text_wide), jnp.bfloat16),) * n_text
        + tuple(pltpu.VMEM((img_rows, wide * len(group)), jnp.bfloat16) for group in groups),
        in_specs=[VMEM] * (2 + bool(groups) + bool(slots)),
        out_specs=(VMEM,) * (n_text + len(groups)),
        scratch_shapes=[
            pltpu.VMEM((max(1, n_text), rows, text_wide), jnp.float32),
            pltpu.VMEM((bm, width), jnp.float32),
        ],
        compiler_params=params(14),
        cost_estimate=cost(microseconds),
        name="gradients",
    )(in_vmem(weights), order, *([in_vmem(texts)] if groups else []), *([in_vmem(images)] if slots else []))


def together(*values):
    return lax.optimization_barrier(values)


def as_bf16_sum(*terms):
    return sum(term.astype(jnp.float32) for term in terms).astype(jnp.bfloat16)


def shifted(count, by):
    return [(i, (i + by) % count) for i in range(count)]


def paired(count, by):
    return [(i, i ^ by) for i in range(count)]


def per_device_4x8(images, texts, positive):
    img_rows = images.shape[0]
    txt_rows, quarter = texts.shape
    width = quarter * 4

    def swap(part, by):
        return lax.ppermute(part, "txt", paired(8, by))

    def over_z(part, by):
        return lax.ppermute(part, "img", paired(4, by))

    def across(part, by_z, by_txt):
        pairs = [(8 * z + c, 8 * (z ^ by_z) + (c ^ by_txt)) for z in range(4) for c in range(8)]
        return lax.ppermute(part, ("img", "txt"), pairs)

    def txt_slot(flip):
        return lambda: lax.axis_index("txt") ^ flip

    def img_slot(by):
        return lambda: lax.rem(lax.axis_index("img") + by, 4)

    targets = (positive - lax.axis_index("txt") * txt_rows).reshape(4, img_rows // 4)
    from_prev = lax.ppermute(texts, "img", shifted(4, 1))
    from_next = lax.ppermute(texts, "img", shifted(4, -1))
    parts = [images, swap(images, 2), swap(images, 4), swap(images, 6)]
    is_first = lax.axis_index("img") == 1
    from_middle = lax.ppermute(jnp.where(is_first, from_prev, from_next), "img", [(1, 2), (2, 1)])
    from_inner = lax.ppermute(jnp.where(is_first, from_next, from_prev), "img", [(1, 0), (2, 3)])
    parts += [swap(part, 1) for part in parts]
    image_pieces = [(part, txt_slot(flip)) for part, flip in zip(parts, (0, 2, 4, 6, 1, 3, 5, 7))]
    text_pieces = [(texts, img_slot(0)), (from_prev, img_slot(3)), (from_next, img_slot(1))]
    most_txt, whole_img, targets = side_by_side(image_pieces, text_pieces, width, targets)
    from_middle, from_inner, most_txt, whole_img = together(from_middle, from_inner, most_txt, whole_img)
    far = ((from_middle, from_inner), img_slot(2), lambda: lax.rem(lax.axis_index("img"), 3) > 0)
    u, row, col, whole_txt = logits_and_stats(whole_img, most_txt, far, targets)

    row = merge_rows(row, swap(row, 1))
    rows = [row] + [swap(row, by) for by in (2, 4, 6)]
    cols = [col] + [over_z(col, by) for by in (1, 2, 3)]

    w, loss, far_grad = weights_and_far(u, whole_img, targets, rows, cols, img_slot(2), quarter, (0, txt_rows))
    middle = lax.ppermute(far_grad, "img", [(1, 2), (2, 1)])
    outer = lax.ppermute(far_grad, "img", [(0, 1), (3, 2)])
    image_groups = [[txt_slot(flip)] for flip in (0, 2, 4, 6)] + [[txt_slot(flip) for flip in (1, 3, 5, 7)]]
    to_next, to_prev, *image_parts = gradients(
        w, whole_img, whole_txt, [img_slot(1), img_slot(3)], quarter, image_groups, row
    )
    loss += across(loss, 1, 1)
    middle, outer, to_next, to_prev, *image_parts, loss = together(
        middle, outer, to_next, to_prev, *image_parts, loss
    )

    other = swap(image_parts.pop(), 1)
    loss += across(loss, 2, 2)
    to_next += jnp.where(is_first, outer, middle)
    to_prev += jnp.where(is_first, middle, outer)
    eighth = width // 8
    s, x, y, d = [part + other[:, j * eighth : (j + 1) * eighth] for j, part in enumerate(image_parts)]
    to_next, to_prev, s, x, y, d, loss = together(to_next, to_prev, s, x, y, d, loss)

    from_prev = lax.ppermute(to_next, "img", shifted(4, 1))
    from_next = lax.ppermute(to_prev, "img", shifted(4, -1))
    own = gradients(w, whole_img, None, [img_slot(0)], quarter, [], loss, 0.01)[0]
    image_grad = as_bf16_sum(s, swap(x, 2), swap(y, 4), swap(d, 6))
    text_grad = as_bf16_sum(own, from_prev, from_next)
    loss = loss[0, 0] + (loss + swap(loss, 4))[0, 1]
    return loss * (ln2 / (2.0 * txt_rows * 8)), image_grad, text_grad


def per_device(images, texts, positive):
    n_img, n_txt = lax.axis_size("img"), lax.axis_size("txt")
    if (n_img, n_txt) == (4, 8):
        return per_device_4x8(images, texts, positive)

    def first_slot():
        return jnp.int32(0)

    def gathered(part, axis):
        every = lax.all_gather(part, axis)
        return [every[k] for k in range(lax.axis_size(axis))]

    whole_img = lax.all_gather(images, "txt", axis=1, tiled=True)
    whole_txt = lax.all_gather(texts, "img", axis=1, tiled=True)
    txt_rows, width = whole_txt.shape
    targets = (positive - lax.axis_index("txt") * txt_rows).reshape(4, whole_img.shape[0] // 4)
    whole_txt, whole_img, targets = side_by_side([(whole_img, first_slot)], [(whole_txt, first_slot)], width, targets)
    u, row, col, whole_txt = logits_and_stats(whole_img, whole_txt, None, targets)
    rows, cols = gathered(row, "txt"), gathered(col, "img")
    w, loss, _ = weights_and_far(u, whole_img, targets, rows, cols, first_slot, 256, (0, txt_rows))
    text_part, image_part = gradients(w, whole_img, whole_txt, [first_slot], width, [[first_slot]], row)
    loss = lax.psum(loss[0, 0] / n_txt + loss[0, 1] / n_img, ("img", "txt"))
    mean_loss = loss * (ln2 / (2.0 * txt_rows * n_txt))
    image_grad = lax.psum_scatter(image_part, "txt", scatter_dimension=1, tiled=True)
    text_grad = lax.psum_scatter(text_part, "img", scatter_dimension=1, tiled=True)
    return mean_loss, image_grad, text_grad


def solution(mesh):
    placed = (P("img", "txt"), P("txt", "img"), P("img"))
    return jax.shard_map(
        per_device,
        mesh=mesh,
        in_specs=placed,
        out_specs=(P(), P("img", "txt"), P("txt", "img")),
        check_vma=False,
    )
```

```python
import functools
import math
import jax
import jax.numpy as jnp
from jax import lax
from jax.experimental import pallas as pl
from jax.experimental.pallas import tpu as pltpu
from jax.sharding import PartitionSpec as P

logit_scale = 100.0
log2e = math.log2(math.e)
ln2 = math.log(2.0)
strip = 16

VMEM = pl.BlockSpec(memory_space=pltpu.VMEM)


def columns(slot, width):
    return pl.ds(pl.multiple_of(slot * width, width), width)


def in_vmem(array):
    return pltpu.with_memory_space_constraint(array, pltpu.VMEM)


def block_of(step, size):
    return pl.ds(pl.multiple_of(step * size, size), size)


def params(mebibytes):
    return pltpu.CompilerParams(vmem_limit_bytes=mebibytes * 1024 * 1024)


def cost(microseconds):
    return pl.CostEstimate(flops=int(1.1e9 * microseconds), bytes_accessed=1, transcendentals=0)


def log_add(*terms):
    larger = functools.reduce(jnp.maximum, terms)
    return larger + jnp.log(sum(jnp.exp2(term - larger) for term in terms)) * log2e


def lanes(x):
    return [x[:, k : k + 128] for k in range(0, x.shape[1], 128)]


def merge_rows(row, other):
    def kernel(row_ref, other_ref, out_ref):
        row, other = row_ref[...], other_ref[...]
        last = lax.broadcasted_iota(jnp.int32, row.shape, 0) == row.shape[0] - 1
        out_ref[...] = jnp.where(last, row + other, log_add(row, other))

    return pl.pallas_call(
        kernel,
        out_shape=jax.ShapeDtypeStruct(row.shape, jnp.float32),
        in_specs=[VMEM, VMEM],
        out_specs=VMEM,
        compiler_params=params(4),
        cost_estimate=cost(0.5),
        name="merge_rows",
    )(row, other)


def side_by_side(image_pieces, text_pieces, width, targets):
    img_rows = image_pieces[0][0].shape[0]
    rows = text_pieces[0][0].shape[0]
    steps = 4
    bm, bt = img_rows // steps, rows // steps
    pieces = text_pieces + image_pieces

    def kernel(*refs):
        *sources, targets_ref, texts_ref, images_ref, spread_ref = refs
        step = pl.program_id(0)
        spread_ref[block_of(step, bm), :] = jnp.broadcast_to(targets_ref[pl.ds(step, 1), :], (128, bm)).T
        texts_ref[block_of(step, bt), :] = jnp.zeros((bt, width), jnp.bfloat16)
        for k, (source, (_, slot)) in enumerate(zip(sources, pieces)):
            target, size = (texts_ref, bt) if k < len(text_pieces) else (images_ref, bm)
            target[block_of(step, size), columns(slot(), source.shape[1])] = source[...]

    return pl.pallas_call(
        kernel,
        grid=(steps,),
        out_shape=(
            pltpu.VMEM((rows, width), jnp.bfloat16),
            pltpu.VMEM((img_rows, width), jnp.bfloat16),
            pltpu.VMEM((img_rows, 128), jnp.int32),
        ),
        in_specs=[pl.BlockSpec((bt, piece.shape[1]), lambda i: (i, 0)) for piece, _ in text_pieces]
        + [pl.BlockSpec((bm, piece.shape[1]), lambda i: (i, 0)) for piece, _ in image_pieces]
        + [VMEM],
        out_specs=(VMEM, VMEM, VMEM),
        compiler_params=params(12),
        cost_estimate=cost(0.01),
        name="side_by_side",
    )(*[piece for piece, _ in pieces], targets)


def logits_and_stats(images, texts, far, targets):
    img_rows, width = images.shape
    rows = texts.shape[0]
    steps = 4
    bm = img_rows // steps
    pieces = rows // 256
    some = bm // pieces

    def kernel(images_ref, texts_ref, targets_ref, *refs):
        if far is not None:
            one_ref, other_ref, *refs = refs
        u_ref, row_ref, col_ref, whole_ref, even_scr, odd_scr, rm_scr, rs_scr, cm_scr, cs_scr, pos_scr = refs
        step = pl.program_id(0)

        @pl.when(step == 0)
        def _():
            cm_scr[...] = jnp.full(cm_scr.shape, -jnp.inf, jnp.float32)
            cs_scr[...] = jnp.zeros(cs_scr.shape, jnp.float32)
            pos_scr[...] = jnp.zeros(pos_scr.shape, jnp.float32)
            whole_ref[...] = texts_ref[...]
            if far is not None:
                whole_ref[:, columns(far[1](), one_ref.shape[1])] = jnp.where(far[2](), one_ref[...], other_ref[...])

        def matmul(j, d_scr):
            at = slice(j * 256, (j + 1) * 256)
            d_scr[:, at] = lax.dot_general(
                images_ref[block_of(step, bm), :], whole_ref[at, :], (((1,), (1,)), ((), ())), preferred_element_type=jnp.float32
            )

        def elementwise(j, d_scr):
            base = (step - 1) * bm
            old = cm_scr[...]
            new = old
            ids = lax.broadcasted_iota(jnp.int32, (strip, 128), 1)
            picked = jnp.zeros((strip, 128), jnp.float32)
            for first in range(j * some, (j + 1) * some, strip):
                at = slice(first, first + strip)
                here = pl.ds(pl.multiple_of(base + first, strip), strip)
                u = d_scr[at, :] * (logit_scale * log2e)
                u_ref[here, :] = u
                target = targets_ref[here, :] - ids
                found = jnp.zeros((strip, 128), jnp.float32)
                for k, v in enumerate(lanes(u)):
                    found = jnp.where(target == 128 * k, v, found)
                picked = picked + found
                rm_scr[at, :] = functools.reduce(jnp.maximum, lanes(u))
                new = jnp.maximum(new, jnp.max(u.reshape(strip // 8, 8, rows), axis=0))
            pos_scr[...] += picked
            cm_scr[...] = new
            total = cs_scr[...] * jnp.exp2(old - new)
            for first in range(j * some, (j + 1) * some, strip):
                at = slice(first, first + strip)
                u = u_ref[pl.ds(pl.multiple_of(base + first, strip), strip), :]
                row_max = rm_scr[at, :]
                rs_scr[at, :] = functools.reduce(jnp.add, [jnp.exp2(v - row_max) for v in lanes(u)])
                total = total + jnp.sum(jnp.exp2(u.reshape(strip // 8, 8, rows) - new[None]), axis=0)
            cs_scr[...] = total

        @pl.when(step == 0)
        def _():
            for j in range(pieces):
                matmul(j, even_scr)

        @pl.when(jnp.logical_and(step < steps, step % 2 == 1))
        def _():
            for j in range(pieces):
                matmul(j, odd_scr)
                elementwise(j, even_scr)

        @pl.when(jnp.logical_and(step > 0, jnp.logical_and(step < steps, step % 2 == 0)))
        def _():
            for j in range(pieces):
                matmul(j, even_scr)
                elementwise(j, odd_scr)

        @pl.when(step == steps)
        def _():
            for j in range(pieces):
                elementwise(j, odd_scr if steps % 2 == 0 else even_scr)

        @pl.when(step > 0)
        def _():
            lane_max, lane_sum = rm_scr[...].T, rs_scr[...].T
            top = jnp.max(lane_max, axis=0, keepdims=True)
            row_sum = jnp.sum(lane_sum * jnp.exp2(lane_max - top), axis=0, keepdims=True)
            row_ref[pl.ds(step - 1, 1), :] = top + jnp.log(row_sum) * log2e

        @pl.when(step == steps)
        def _():
            top = jnp.max(cm_scr[...], axis=0, keepdims=True)
            col_sum = jnp.sum(cs_scr[...] * jnp.exp2(cm_scr[...] - top), axis=0, keepdims=True)
            col_ref[...] = top + jnp.log(col_sum) * log2e
            row_ref[pl.ds(steps, 1), :] = jnp.full((1, bm), jnp.sum(pos_scr[...]))

    return pl.pallas_call(
        kernel,
        grid=(steps + 1,),
        out_shape=(
            pltpu.VMEM((img_rows, rows), jnp.float32),
            jax.ShapeDtypeStruct((steps + 1, bm), jnp.float32),
            jax.ShapeDtypeStruct((1, rows), jnp.float32),
            pltpu.VMEM((rows, width), jnp.bfloat16),
        ),
        in_specs=[VMEM] * (3 if far is None else 5),
        out_specs=(VMEM,) * 4,
        scratch_shapes=[
            pltpu.VMEM((bm, rows), jnp.float32),
            pltpu.VMEM((bm, rows), jnp.float32),
            pltpu.VMEM((bm, 128), jnp.float32),
            pltpu.VMEM((bm, 128), jnp.float32),
            pltpu.VMEM((8, rows), jnp.float32),
            pltpu.VMEM((8, rows), jnp.float32),
            pltpu.VMEM((strip, 128), jnp.float32),
        ],
        compiler_params=params(12),
        cost_estimate=cost(13),
        name="logits_and_stats",
    )(in_vmem(images), in_vmem(texts), in_vmem(targets), *(() if far is None else map(in_vmem, far[0])))


def weights_and_far(u, images, targets, row_lses, col_lses, slot, wide, cuts):
    img_rows = images.shape[0]
    rows = u.shape[1]
    steps = 4
    bm = img_rows // steps
    n_row, n_col = len(row_lses), len(col_lses)
    groups = [(first, min(first + 256, bm)) for first in range(0, bm, 256)]

    def kernel(u_ref, images_ref, targets_ref, *refs):
        row_refs, col_refs, refs = refs[:n_row], refs[n_row : n_row + n_col], refs[n_row + n_col :]
        w_ref, loss_ref, *refs = refs
        far_refs, refs = refs[: len(cuts) - 1], refs[len(cuts) - 1 :]
        group_scrs, (acc, row_ref, col_ref, row_scr) = refs[: len(groups)], refs[len(groups) :]
        step = pl.program_id(0)

        @pl.when(step == 0)
        def _():
            acc[...] = jnp.zeros(acc.shape, jnp.float32)
            row_ref[...] = log_add(*[ref[:steps, :] for ref in row_refs])
            col_ref[...] = log_add(*[ref[...] for ref in col_refs])
            picked = sum(ref[steps:, :1] for ref in row_refs)
            row_loss = jnp.sum(row_ref[...], keepdims=True) - 2.0 * picked
            col_loss = jnp.sum(col_ref[...], keepdims=True)
            lane = lax.broadcasted_iota(jnp.int32, (1, 128), 1)
            loss_ref[...] = jnp.where(lane == 0, row_loss, jnp.where(lane == 1, col_loss, 0.0))

        row_scr[...] = jnp.broadcast_to(row_ref[pl.ds(step, 1), :], (128, bm)).T
        ids = lax.broadcasted_iota(jnp.int32, (strip, 128), 1)
        col = col_ref[...]
        for (group, end), w_scr in zip(groups, group_scrs):
            rows_here = pl.ds(pl.multiple_of(step * bm + group, 128), end - group)
            for first in range(group, end, strip):
                at = slice(first, first + strip)
                here = pl.ds(pl.multiple_of(step * bm + first, strip), strip)
                row = row_scr[at, :]
                target = targets_ref[here, :] - ids
                for k in range(0, rows, 128):
                    v = u_ref[here, k : k + 128]
                    weight = jnp.exp2(v - row) + jnp.exp2(v - col[:, k : k + 128]) - jnp.where(target == k, 2.0, 0.0)
                    weight = weight.astype(jnp.bfloat16)
                    w_ref[here, k : k + 128] = weight
                    w_scr[first - group : first - group + strip, k : k + 128] = weight
            acc[...] += lax.dot_general(
                w_scr[...],
                images_ref[rows_here, columns(slot(), wide)],
                (((0,), (0,)), ((), ())),
                preferred_element_type=jnp.float32,
            )

        @pl.when(step == steps - 1)
        def _():
            for far_ref, first, end in zip(far_refs, cuts, cuts[1:]):
                far_ref[...] = (logit_scale * acc[first:end, :]).astype(jnp.bfloat16)

    return pl.pallas_call(
        kernel,
        grid=(steps,),
        out_shape=(
            pltpu.VMEM((img_rows, rows), jnp.bfloat16),
            jax.ShapeDtypeStruct((1, 128), jnp.float32),
        )
        + tuple(pltpu.VMEM((end - first, wide), jnp.bfloat16) for first, end in zip(cuts, cuts[1:])),
        in_specs=[VMEM] * (3 + n_row + n_col),
        out_specs=(VMEM,) * (len(cuts) + 1),
        scratch_shapes=[pltpu.VMEM((end - first, rows), jnp.bfloat16) for first, end in groups]
        + [
            pltpu.VMEM((rows, wide), jnp.float32),
            pltpu.VMEM((steps, bm), jnp.float32),
            pltpu.VMEM((1, rows), jnp.float32),
            pltpu.VMEM((bm, 128), jnp.float32),
        ],
        compiler_params=params(8),
        cost_estimate=cost(8),
        name="weights_and_far",
    )(in_vmem(u), in_vmem(images), in_vmem(targets), *map(in_vmem, row_lses), *map(in_vmem, col_lses))


def gradients(weights, images, texts, slots, text_wide, groups, order, microseconds=10):
    img_rows, rows = weights.shape
    width = images.shape[1]
    steps = 4
    bm = img_rows // steps
    wide = width // max(1, sum(len(group) for group in groups))
    n_text = len(slots)

    def kernel(w_ref, _, *refs):
        if groups:
            texts_ref, *refs = refs
        if slots:
            images_ref, *refs = refs
        text_outs, (*image_outs, acc, image_acc) = refs[:n_text], refs[n_text:]
        step = pl.program_id(0)
        here = block_of(step, bm)

        if slots:

            @pl.when(step == 0)
            def _():
                acc[...] = jnp.zeros(acc.shape, jnp.float32)

        for k, slot in enumerate(slots):
            acc[k] += lax.dot_general(
                w_ref[here, :],
                images_ref[here, columns(slot(), text_wide)],
                (((0,), (0,)), ((), ())),
                preferred_element_type=jnp.float32,
            )
        if groups:
            image_acc[...] = logit_scale * jnp.dot(
                w_ref[here, :], texts_ref[...], preferred_element_type=jnp.float32
            )
        for out, group in zip(image_outs, groups):
            for k, slot in enumerate(group):
                out[here, k * wide : (k + 1) * wide] = image_acc[:, columns(slot(), wide)].astype(jnp.bfloat16)

        @pl.when(step == steps - 1)
        def _():
            for k, out in enumerate(text_outs):
                out[...] = (logit_scale * acc[k]).astype(jnp.bfloat16)

    return pl.pallas_call(
        kernel,
        grid=(steps,),
        out_shape=(pltpu.VMEM((rows, text_wide), jnp.bfloat16),) * n_text
        + tuple(pltpu.VMEM((img_rows, wide * len(group)), jnp.bfloat16) for group in groups),
        in_specs=[VMEM] * (2 + bool(groups) + bool(slots)),
        out_specs=(VMEM,) * (n_text + len(groups)),
        scratch_shapes=[
            pltpu.VMEM((max(1, n_text), rows, text_wide), jnp.float32),
            pltpu.VMEM((bm, width), jnp.float32),
        ],
        compiler_params=params(14),
        cost_estimate=cost(microseconds),
        name="gradients",
    )(in_vmem(weights), order, *([in_vmem(texts)] if groups else []), *([in_vmem(images)] if slots else []))


def together(*values):
    return lax.optimization_barrier(values)


def as_bf16_sum(*terms):
    return sum(term.astype(jnp.float32) for term in terms).astype(jnp.bfloat16)


def shifted(count, by):
    return [(i, (i + by) % count) for i in range(count)]


def paired(count, by):
    return [(i, i ^ by) for i in range(count)]


def per_device_4x8(images, texts, positive):
    img_rows = images.shape[0]
    txt_rows, quarter = texts.shape
    width = quarter * 4

    def swap(part, by):
        return lax.ppermute(part, "txt", paired(8, by))

    def over_z(part, by):
        return lax.ppermute(part, "img", paired(4, by))

    def across(part, by_z, by_txt):
        pairs = [(8 * z + c, 8 * (z ^ by_z) + (c ^ by_txt)) for z in range(4) for c in range(8)]
        return lax.ppermute(part, ("img", "txt"), pairs)

    def txt_slot(flip):
        return lambda: lax.axis_index("txt") ^ flip

    def img_slot(by):
        return lambda: lax.rem(lax.axis_index("img") + by, 4)

    targets = (positive - lax.axis_index("txt") * txt_rows).reshape(4, img_rows // 4)
    from_prev = lax.ppermute(texts, "img", shifted(4, 1))
    from_next = lax.ppermute(texts, "img", shifted(4, -1))
    parts = [images, swap(images, 2), swap(images, 4), swap(images, 6)]
    is_first = lax.axis_index("img") == 1
    from_middle = lax.ppermute(jnp.where(is_first, from_prev, from_next), "img", [(1, 2), (2, 1)])
    from_inner = lax.ppermute(jnp.where(is_first, from_next, from_prev), "img", [(1, 0), (2, 3)])
    parts += [swap(part, 1) for part in parts]
    image_pieces = [(part, txt_slot(flip)) for part, flip in zip(parts, (0, 2, 4, 6, 1, 3, 5, 7))]
    text_pieces = [(texts, img_slot(0)), (from_prev, img_slot(3)), (from_next, img_slot(1))]
    most_txt, whole_img, targets = side_by_side(image_pieces, text_pieces, width, targets)
    from_middle, from_inner, most_txt, whole_img = together(from_middle, from_inner, most_txt, whole_img)
    far = ((from_middle, from_inner), img_slot(2), lambda: lax.rem(lax.axis_index("img"), 3) > 0)
    u, row, col, whole_txt = logits_and_stats(whole_img, most_txt, far, targets)

    row = merge_rows(row, swap(row, 1))
    rows = [row] + [swap(row, by) for by in (2, 4, 6)]
    cols = [col] + [over_z(col, by) for by in (1, 2, 3)]

    w, loss, far_grad = weights_and_far(u, whole_img, targets, rows, cols, img_slot(2), quarter, (0, txt_rows))
    middle = lax.ppermute(far_grad, "img", [(1, 2), (2, 1)])
    outer = lax.ppermute(far_grad, "img", [(0, 1), (3, 2)])
    image_groups = [[txt_slot(flip)] for flip in (0, 2, 4, 6)] + [[txt_slot(flip) for flip in (1, 3, 5, 7)]]
    to_next, to_prev, *image_parts = gradients(
        w, whole_img, whole_txt, [img_slot(1), img_slot(3)], quarter, image_groups, row
    )
    loss += across(loss, 1, 1)
    middle, outer, to_next, to_prev, *image_parts, loss = together(
        middle, outer, to_next, to_prev, *image_parts, loss
    )

    other = swap(image_parts.pop(), 1)
    loss += across(loss, 2, 2)
    to_next += jnp.where(is_first, outer, middle)
    to_prev += jnp.where(is_first, middle, outer)
    eighth = width // 8
    s, x, y, d = [part + other[:, j * eighth : (j + 1) * eighth] for j, part in enumerate(image_parts)]
    to_next, to_prev, s, x, y, d, loss = together(to_next, to_prev, s, x, y, d, loss)

    from_prev = lax.ppermute(to_next, "img", shifted(4, 1))
    from_next = lax.ppermute(to_prev, "img", shifted(4, -1))
    own = gradients(w, whole_img, None, [img_slot(0)], quarter, [], loss, 0.01)[0]
    image_grad = as_bf16_sum(s, swap(x, 2), swap(y, 4), swap(d, 6))
    text_grad = as_bf16_sum(own, from_prev, from_next)
    loss = loss[0, 0] + (loss + swap(loss, 4))[0, 1]
    return loss * (ln2 / (2.0 * txt_rows * 8)), image_grad, text_grad


def per_device(images, texts, positive):
    n_img, n_txt = lax.axis_size("img"), lax.axis_size("txt")
    if (n_img, n_txt) == (4, 8):
        return per_device_4x8(images, texts, positive)

    def first_slot():
        return jnp.int32(0)

    def gathered(part, axis):
        every = lax.all_gather(part, axis)
        return [every[k] for k in range(lax.axis_size(axis))]

    whole_img = lax.all_gather(images, "txt", axis=1, tiled=True)
    whole_txt = lax.all_gather(texts, "img", axis=1, tiled=True)
    txt_rows, width = whole_txt.shape
    targets = (positive - lax.axis_index("txt") * txt_rows).reshape(4, whole_img.shape[0] // 4)
    whole_txt, whole_img, targets = side_by_side([(whole_img, first_slot)], [(whole_txt, first_slot)], width, targets)
    u, row, col, whole_txt = logits_and_stats(whole_img, whole_txt, None, targets)
    rows, cols = gathered(row, "txt"), gathered(col, "img")
    w, loss, _ = weights_and_far(u, whole_img, targets, rows, cols, first_slot, 256, (0, txt_rows))
    text_part, image_part = gradients(w, whole_img, whole_txt, [first_slot], width, [[first_slot]], row)
    loss = lax.psum(loss[0, 0] / n_txt + loss[0, 1] / n_img, ("img", "txt"))
    mean_loss = loss * (ln2 / (2.0 * txt_rows * n_txt))
    image_grad = lax.psum_scatter(image_part, "txt", scatter_dimension=1, tiled=True)
    text_grad = lax.psum_scatter(text_part, "img", scatter_dimension=1, tiled=True)
    return mean_loss, image_grad, text_grad


def solution(mesh):
    placed = (P("img", "txt"), P("txt", "img"), P("img"))
    return jax.shard_map(
        per_device,
        mesh=mesh,
        in_specs=placed,
        out_specs=(P(), P("img", "txt"), P("txt", "img")),
        check_vma=False,
    )
```
